512 devices in a mesh: dp: 4 (over y), sx: 8 (over z_lo), sy: 16 (over z_hi, x, core).
Axes of the slice: x: 4, y: 4, z: 16 (z_hi: 2, z_lo: 8; z = z_hi * 8 + z_lo), core: 2. Of those that a mesh axis runs over, the one named last changes fastest.
Arguments:
- volume: bfloat16 [4, 4, 64, 128, 128], P('dp', None, 'sx', 'sy'), may hold values from -6 to 6
- cotangent: bfloat16 [4, 256, 8, 16, 16], P('dp', ('sx', 'sy')), may hold values from -0.119628906 to 0.119628906
- first_weight: bfloat16 [3, 3, 3, 4, 64], replicated, may hold values from -0.625 to 0.625
- second_weight: bfloat16 [3, 3, 3, 64, 64], replicated, may hold values from -0.15625 to 0.15625
- third_weight: bfloat16 [3, 3, 3, 64, 256], replicated, may hold values from -0.15625 to 0.15625
Outputs:
- grad_first: float32 [3, 3, 3, 4, 64], replicated
- grad_second: float32 [3, 3, 3, 64, 64], replicated
- grad_third: float32 [3, 3, 3, 64, 256], replicated
The draws below stay inside these ranges and needn't reach their ends.
All inputs are finite; a program needn't handle non-finite values.
Results may differ from the reference program's by a relative error of at most 0.014.
Values may be sent and summed in bfloat16 or wider, within the bound.
A program may use at most 128 MiB of HBM per device.

```python
import jax
import jax.numpy as jnp
from jax import lax

CIN = 4
C1 = 64
C3 = 256
NZ = 128
BATCH = 4
NX = 64
NY = 128


def levels(own_key, shape, pieces, smallest, largest):
    loudness, own = 1.0, jax.random.fold_in(own_key, 6)
    for dim, shards_of in pieces:
        steps = jnp.exp(jax.random.uniform(jax.random.fold_in(own, dim), (shards_of,), jnp.float32, smallest / len(pieces), largest / len(pieces)))
        loudness = loudness * jnp.repeat(steps, shape[dim] // shards_of).reshape([-1 if axis == dim else 1 for axis in range(len(shape))])
    return loudness


def gaussian(own_key, extent, spread, most, split=(), held_as=jnp.bfloat16):
    result = jax.random.normal(own_key, extent, jnp.float32) * spread
    if len(split) > 0:
        result = levels(own_key, extent, split, -0.22, 0.18) * result
    return jnp.clip(result, min=-most, max=most).astype(held_as)


def setup_inputs(seed: int = 0) -> dict:
    arg_keys = jax.random.split(jax.random.key(seed), 6)
    volume = gaussian(arg_keys[0], (BATCH, CIN, NX, NY, NZ), 1.0, 6.0, ((0, 4), (2, 8), (3, 16)))
    cotangent = gaussian(arg_keys[1], (BATCH, C3, NX // 8, NY // 8, NZ // 8), 0.02, 0.119628906, ((0, 4), (1, 128)))
    first_weight = gaussian(arg_keys[2], (3, 3, 3, CIN, C1), (27 * CIN) ** -0.5, 0.625)
    second_weight = gaussian(arg_keys[3], (3, 3, 3, C1, C1), (27 * C1) ** -0.5, 0.15625)
    third_weight = gaussian(arg_keys[4], (3, 3, 3, C1, C3), (27 * C1) ** -0.5, 0.15625)
    return {"volume": volume, "cotangent": cotangent, "first_weight": first_weight, "second_weight": second_weight, "third_weight": third_weight}


LAYOUT = ('NCDHW', 'DHWIO', 'NCDHW')

def convolve(field, kernel, margins):
    return lax.conv_general_dilated(field, kernel, (2, 2, 2), margins, dimension_numbers=LAYOUT, precision=lax.Precision.HIGHEST)

def gelu_back(preact, upstream):
    return jax.vjp(jax.nn.gelu, preact)[1](upstream)[0]

def settle(values):
    return lax.optimization_barrier(values.astype(jnp.bfloat16))

def reference(volume, cotangent, first_weight, second_weight, third_weight):
    margins = ((1, 1), (1, 1), (1, 1))
    first_kernel = first_weight.astype(jnp.float32)
    second_kernel = second_weight.astype(jnp.float32)
    third_kernel = third_weight.astype(jnp.float32)
    source = volume.astype(jnp.float32)
    pre_first, pull_first = jax.vjp(lambda kernel: convolve(source, kernel, margins), first_kernel)
    act_first = settle(jax.nn.gelu(pre_first))
    pre_second, pull_second = jax.vjp(lambda field, kernel: convolve(field, kernel, margins), act_first.astype(jnp.float32), second_kernel)
    act_second = settle(jax.nn.gelu(pre_second))
    pre_third, pull_third = jax.vjp(lambda field, kernel: convolve(field, kernel, margins), act_second.astype(jnp.float32), third_kernel)
    delta_third = settle(gelu_back(pre_third, cotangent.astype(jnp.float32)))
    back_second, grad_third = pull_third(delta_third.astype(jnp.float32))
    delta_second = settle(gelu_back(pre_second, back_second))
    back_first, grad_second = pull_second(delta_second.astype(jnp.float32))
    delta_first = settle(gelu_back(pre_first, back_first))
    grad_first = pull_first(delta_first.astype(jnp.float32))[0]
    return (grad_first, grad_second, grad_third)
```

```python
import functools
import math

import jax
import jax.numpy as jnp
from jax import lax
from jax.experimental import pallas as pl
from jax.experimental.pallas import tpu as pltpu
from jax.sharding import PartitionSpec as P

MESH = pl.DeviceIdType.MESH
CORES = 2
ROWS, LANES = 16, 128

LAYOUT = ("NCDHW", "DHWIO", "NCDHW")
ADJOINT_LAYOUT = ("NCDHW", "DHWOI", "NCDHW")


def passed_along(value, axis, steps):
    count = lax.axis_size(axis)
    leading, last = (max(0, -steps), min(count, count - steps))
    return lax.ppermute(value, axis, [(source, source + steps) for source in range(leading, last)])


def convolve(field, kernel, margins):
    return lax.conv_general_dilated(
        field,
        kernel,
        (2, 2, 2),
        margins,
        dimension_numbers=LAYOUT,
        preferred_element_type=jnp.float32,
    )


def kernel_grad(field, delta, margins):
    padded = jnp.pad(field, ((0, 0), (0, 0)) + tuple(margins))
    samples = field.shape[0]
    channels_in = field.shape[1]
    out_x, out_y, out_z = (delta.shape[2], delta.shape[3], delta.shape[4])
    tap_terms = []
    for shift_x in range(3):
        for shift_y in range(3):
            for shift_z in range(3):
                window = lax.slice(
                    padded,
                    (0, 0, shift_x, shift_y, shift_z),
                    (
                        samples,
                        channels_in,
                        shift_x + 2 * out_x - 1,
                        shift_y + 2 * out_y - 1,
                        shift_z + 2 * out_z - 1,
                    ),
                    (1, 1, 2, 2, 2),
                )
                tap_terms.append(
                    jnp.einsum("bcxyz,boxyz->co", window, delta, preferred_element_type=jnp.float32)
                )
    return jnp.stack(tap_terms).reshape(3, 3, 3, channels_in, delta.shape[1])


def adjoint(delta, kernel, lower_pads, lengths):
    borders = []
    for lower_pad, length, cell_count in zip(lower_pads, lengths, delta.shape[2:]):
        borders.append((2 - lower_pad, length + 1 + lower_pad - 2 * cell_count))
    flipped = kernel[::-1, ::-1, ::-1]
    return lax.conv_general_dilated(
        delta,
        flipped,
        (1, 1, 1),
        borders,
        lhs_dilation=(2, 2, 2),
        dimension_numbers=ADJOINT_LAYOUT,
        preferred_element_type=jnp.float32,
    )


def gelu_back(preact, upstream):
    return jax.vjp(jax.nn.gelu, preact)[1](upstream)[0]


def settle(values):
    return values.astype(jnp.bfloat16)


def rim_along_x(plane):
    return passed_along(plane, "sx", 1)


def rim_along_y(plane):
    return passed_along(plane, "sy", 1)


def late_rim_x(plane):
    return passed_along(plane, "sx", 1)


def late_rim_y(plane):
    return passed_along(plane, "sy", 1)


def extend(field, along_x, along_y):
    below = along_x(field[:, :, -1:])
    wider = jnp.concatenate([below, field], axis=2)
    beside = along_y(wider[:, :, :, -1:])
    return jnp.concatenate([beside, wider], axis=3)


def retract(gradient):
    upper_side = passed_along(gradient[:, :, :, :1].astype(jnp.bfloat16), "sy", -1).astype(
        jnp.float32
    )
    interior = gradient[:, :, :, 1:]
    interior = interior.at[:, :, :, -1:].add(upper_side)
    upper_row = passed_along(interior[:, :, :1].astype(jnp.bfloat16), "sx", -1).astype(jnp.float32)
    kept_cells = interior[:, :, 1:]
    return kept_cells.at[:, :, -1:].add(upper_row)


def to_blocks(values, blocks_x, blocks_y):
    samples, channels, extent_x, extent_y, extent_z = values.shape
    width_x = extent_x // blocks_x
    width_y = extent_y // blocks_y
    pieces = values.reshape(samples, channels, blocks_x, width_x, blocks_y, width_y, extent_z)
    pieces = pieces.transpose(2, 4, 0, 1, 3, 5, 6).reshape(
        blocks_x * blocks_y, samples, channels, width_x, width_y, extent_z
    )
    arrived = lax.all_to_all(pieces, ("sx", "sy"), split_axis=0, concat_axis=2, tiled=True)
    return arrived[0]


class Place:
    def __init__(self, dp, sx, sy):
        self.cores = CORES
        self.chips_x = min(4, sy // CORES)
        self.high_z = sy // (CORES * self.chips_x)
        self.low_z, self.chips_y = sx, dp
        self.plane = self.chips_x * self.chips_y
        self.depth = self.high_z * self.low_z
        y, low, mixed = (lax.axis_index(name) for name in ("dp", "sx", "sy"))
        self.core = lax.rem(mixed, CORES)
        chip_x = lax.rem(mixed // CORES, self.chips_x)
        self.p = chip_x * self.chips_y + y
        self.z = (mixed // (CORES * self.chips_x)) * self.low_z + low

    def device(self, core=None, p=None, z=None):
        core = self.core if core is None else core
        p = self.p if p is None else p
        z = self.z if z is None else z
        chip_x, y = p // self.chips_y, lax.rem(p, self.chips_y)
        high, low = z // self.low_z, lax.rem(z, self.low_z)
        return (y, low, (high * self.chips_x + chip_x) * CORES + core)


def others(count, me, body):
    def step(distance, carry):
        body(lax.rem(me + distance, count))
        return carry

    lax.fori_loop(1, count, step, 0)


def reduce_kernel(sizes, grads, total, half_out, half_in, plane_out, plane_in, depth_out, depth_in,
                  final, gathered, half_sems, plane_sems, depth_sems, final_sems, gather_sems, pair_sems):
    here = Place(*sizes)
    plane, depth = here.plane, here.depth
    share = plane_out.shape[1]
    half = plane * share
    owners = [unit * depth // share for unit in range(share)]

    barrier = pltpu.get_barrier_semaphore()

    def greet(device):
        pl.semaphore_signal(barrier, inc=1, device_id=device, device_id_type=MESH)

    greet(here.device(core=1 - here.core))
    others(plane, here.p, lambda q: greet(here.device(p=q)))
    others(depth, here.z, lambda q: greet(here.device(z=q)))
    pl.semaphore_wait(barrier, 1 + (plane - 1) + (depth - 1))

    def copy(source, target, sems, at, there, device):
        return pltpu.make_async_remote_copy(
            src_ref=source, dst_ref=target, send_sem=sems.at[0, at], recv_sem=sems.at[1, there],
            device_id=device, device_id_type=MESH)

    mine, yours = here.core * half, (1 - here.core) * half
    partner = here.device(core=1 - here.core)
    half_out[...] = grads[pl.ds(yours, half)].astype(jnp.bfloat16)
    swap = copy(half_out, half_in, half_sems, 0, 0, partner)
    swap.start()
    swap.wait()
    plane_out[...] = (
        grads[pl.ds(mine, half)] + half_in[...].astype(jnp.float32)
    ).astype(jnp.bfloat16).reshape(plane_out.shape)

    def to_plane(q):
        copy(plane_out.at[q], plane_in.at[here.p], plane_sems, q, here.p, here.device(p=q)).start()

    def from_plane(q):
        copy(plane_out.at[q], plane_in.at[q], plane_sems, q, q, here.device(p=q)).wait()

    others(plane, here.p, to_plane)
    plane_in[here.p] = plane_out[here.p]
    others(plane, here.p, from_plane)
    depth_out[...] = jnp.sum(plane_in[...].astype(jnp.float32), axis=0).astype(jnp.bfloat16)

    for unit, owner in enumerate(owners):
        @pl.when(here.z != owner)
        def _():
            copy(depth_out.at[unit], depth_in.at[here.z], depth_sems, unit, here.z, here.device(z=owner)).start()

    for unit, owner in enumerate(owners):
        @pl.when(here.z == owner)
        def _():
            depth_in[owner] = depth_out[unit]

            def arrive(q):
                copy(depth_out.at[unit], depth_in.at[q], depth_sems, unit, q, here.device(z=q)).wait_recv()

            others(depth, here.z, arrive)
            final[unit] = jnp.sum(depth_in[...].astype(jnp.float32), axis=0).astype(jnp.bfloat16)

            def share_it(q):
                copy(final.at[unit], final.at[unit], final_sems, q, depth + unit, here.device(z=q)).start()

            others(depth, here.z, share_it)

    for unit, owner in enumerate(owners):
        @pl.when(here.z != owner)
        def _():
            copy(depth_out.at[unit], depth_in.at[here.z], depth_sems, unit, here.z, here.device(z=owner)).wait_send()
            copy(final.at[unit], final.at[unit], final_sems, unit, depth + unit, here.device(z=owner)).wait_recv()

    def to_gather(q):
        copy(final, gathered.at[here.core, here.p], gather_sems, q, here.p, here.device(p=q)).start()

    others(plane, here.p, to_gather)
    gathered[here.core, here.p] = final[...]

    def pair(q):
        return copy(gathered.at[here.core, q], gathered.at[here.core, q], pair_sems, q, q, partner)

    pair(here.p).start()

    def pass_on(q):
        copy(final, gathered.at[here.core, q], gather_sems, q, q, here.device(p=q)).wait_recv()
        pair(q).start()

    others(plane, here.p, pass_on)

    for unit, owner in enumerate(owners):
        @pl.when(here.z == owner)
        def _():
            def sent(q):
                copy(final.at[unit], final.at[unit], final_sems, q, depth + unit, here.device(z=q)).wait_send()

            others(depth, here.z, sent)

    others(plane, here.p, lambda q: copy(final, gathered.at[here.core, q], gather_sems, q, q, here.device(p=q)).wait_send())

    def arrived(q, carry):
        copy(gathered.at[1 - here.core, q], gathered.at[1 - here.core, q], pair_sems, q, q, partner).wait()
        return carry

    lax.fori_loop(0, plane, arrived, 0)
    total[...] = gathered[...].astype(jnp.float32).reshape(total.shape)


def summed(sizes, grads):
    plane, depth = min(4, sizes[2] // CORES) * sizes[0], sizes[1] * max(1, sizes[2] // (4 * CORES))
    share = grads.shape[0] // (CORES * plane)
    half = plane * share
    low = jnp.bfloat16
    return pl.pallas_call(
        functools.partial(reduce_kernel, sizes),
        out_shape=jax.ShapeDtypeStruct(grads.shape, jnp.float32),
        in_specs=[pl.BlockSpec(memory_space=pltpu.VMEM)],
        out_specs=pl.BlockSpec(memory_space=pltpu.VMEM),
        scratch_shapes=[
            pltpu.VMEM((half, ROWS, LANES), low),
            pltpu.VMEM((half, ROWS, LANES), low),
            pltpu.VMEM((plane, share, ROWS, LANES), low),
            pltpu.VMEM((plane, share, ROWS, LANES), low),
            pltpu.VMEM((share, ROWS, LANES), low),
            pltpu.VMEM((depth, ROWS, LANES), low),
            pltpu.VMEM((share, ROWS, LANES), low),
            pltpu.VMEM((CORES, plane, share, ROWS, LANES), low),
            pltpu.SemaphoreType.DMA((2, 1)),
            pltpu.SemaphoreType.DMA((2, plane)),
            pltpu.SemaphoreType.DMA((2, max(depth, share))),
            pltpu.SemaphoreType.DMA((2, depth + share)),
            pltpu.SemaphoreType.DMA((2, plane)),
            pltpu.SemaphoreType.DMA((2, plane)),
        ],
        compiler_params=pltpu.CompilerParams(
            collective_id=1, has_side_effects=True, vmem_limit_bytes=40 * 2**20),
        cost_estimate=pl.CostEstimate(flops=0, bytes_accessed=5_000_000, transcendentals=0),
    )(grads)


def sum_all(sizes, parts):
    shapes = [part.shape for part in parts]
    counts = [math.prod(shape) for shape in shapes]
    grain = ROWS * LANES * CORES * min(4, sizes[2] // CORES) * sizes[0]
    flat = jnp.concatenate([part.reshape(-1) for part in parts])
    flat = jnp.pad(flat, (0, -flat.shape[0] % grain))
    out = summed(sizes, flat.reshape(-1, ROWS, LANES)).reshape(-1)
    results, offset = [], 0
    for shape, count in zip(shapes, counts):
        results.append(out[offset:offset + count].reshape(shape))
        offset += count
    return tuple(results)


def local(volume, cotangent, first_weight, second_weight, third_weight):
    block_margins = ((0, 0), (0, 0), (1, 1))
    lower_block = (0, 0, 1)
    blocks_x = lax.axis_size("sx")
    blocks_y = lax.axis_size("sy")
    source = extend(volume, rim_along_x, rim_along_y)
    pre_first = convolve(source, first_weight, block_margins)
    act_first = settle(jax.nn.gelu(pre_first))
    padded_first = extend(act_first, rim_along_x, rim_along_y)
    pre_second = convolve(padded_first, second_weight, block_margins)
    act_second = settle(jax.nn.gelu(pre_second))
    padded_second = extend(act_second, late_rim_x, late_rim_y)
    upstream = to_blocks(cotangent, blocks_x, blocks_y)
    pre_third = convolve(padded_second, third_weight, block_margins)
    delta_third = settle(gelu_back(pre_third, upstream.astype(jnp.float32)))
    grad_third = kernel_grad(padded_second, delta_third, block_margins)
    back_padded = adjoint(delta_third, third_weight, lower_block, padded_second.shape[2:])
    back_second = retract(back_padded)
    delta_second = settle(gelu_back(pre_second, back_second))
    grad_second = kernel_grad(padded_first, delta_second, block_margins)
    back_first = retract(adjoint(delta_second, second_weight, lower_block, padded_first.shape[2:]))
    delta_first = settle(gelu_back(pre_first, back_first))
    grad_first = kernel_grad(source, delta_first, block_margins)
    sizes = (lax.axis_size("dp"), blocks_x, blocks_y)
    return sum_all(sizes, (grad_first, grad_second, grad_third))


def solution(mesh):
    placed = (
        P("dp", None, "sx", "sy", None),
        P("dp", ("sx", "sy"), None, None, None),
        P(),
        P(),
        P(),
    )
    return jax.shard_map(
        local, mesh=mesh, in_specs=placed, out_specs=(P(), P(), P()), check_vma=False
    )
```

```python
import functools

import jax
import jax.numpy as jnp
import numpy as np
from jax import lax
from jax.experimental import pallas as pl
from jax.experimental.pallas import tpu as pltpu
from jax.sharding import PartitionSpec as P

MESH = pl.DeviceIdType.MESH
LOW, WIDE = jnp.bfloat16, jnp.float32
CORES = 2
ROWS, LANES = 16, 128
SLOT = 40
FIRST_UNITS, SECOND_UNITS, THIRD_UNITS = 8, 56, 216
OWN = ((0, 0), (0, 1), (1, 0), (1, 1))
CELLS = [(1 + a, 1 + b) for a, b in OWN] + [(0, 0), (0, 1), (0, 2), (1, 0), (2, 0)]


def selection():
    result = np.zeros((3, 2, 2, 4, 16, 7, LANES), np.float32)
    for offset in range(3):
        for dx, (pair, odd) in enumerate(((1, 1), (0, 0), (0, 1))):
            for channel in range(4):
                for cell in range(7):
                    for dy in range(3):
                        lane = offset * SLOT + (dx * 3 + dy) * 4 + channel
                        result[offset, pair, odd, channel, 2 * cell + dy + 1, cell, lane] = 1
    return result.reshape(768, 7 * LANES)


def gelu_parts(v):
    square = v * v
    t = jnp.tanh(np.sqrt(2 / np.pi) * (v + 0.044715 * (v * square)))
    return t, square


def gelu(v):
    t, _ = gelu_parts(v)
    return 0.5 * v * (1 + t)


def gelu_slope(v):
    t, square = gelu_parts(v)
    return 0.5 * (1 + t) + 0.5 * v * (1 - t * t) * (np.sqrt(2 / np.pi) * (1 + 3 * 0.044715 * square))


def dot(a, b, transposed=False):
    return lax.dot_general(a, b, (((1,), (1 if transposed else 0,)), ((), ())), preferred_element_type=WIDE)


def down(v, period):
    row = lax.broadcasted_iota(jnp.int32, v.shape, 0)
    return jnp.where((row & (period - 1)) == 0, 0.0, pltpu.roll(v, 1, axis=0))


def up(v):
    row = lax.broadcasted_iota(jnp.int32, v.shape, 0)
    return jnp.where(row == v.shape[0] - 1, 0.0, pltpu.roll(v, v.shape[0] - 1, axis=0))


class Place:
    def __init__(self, dp, sx, sy):
        self.chips_x = min(4, sy // CORES)
        self.low_z, self.chips_y = sx, dp
        self.plane = self.chips_x * dp
        self.depth = sx * (sy // (CORES * self.chips_x))
        self.y, self.sx, self.sy = (lax.axis_index(name) for name in ("dp", "sx", "sy"))
        self.core = lax.rem(self.sy, CORES)
        self.p = lax.rem(self.sy // CORES, self.chips_x) * dp + self.y
        self.z = (self.sy // (CORES * self.chips_x)) * sx + self.sx

    def device(self, core=None, p=None, z=None):
        core = self.core if core is None else core
        p = self.p if p is None else p
        z = self.z if z is None else z
        chip_x, y = p // self.chips_y, lax.rem(p, self.chips_y)
        high, low = z // self.low_z, lax.rem(z, self.low_z)
        return (y, low, (high * self.chips_x + chip_x) * CORES + core)


def others(count, me, body):
    def step(distance, carry):
        body(lax.rem(me + distance, count))
        return carry

    lax.fori_loop(1, count, step, 0)


def copy(source, target, sems, at, there, device):
    return pltpu.make_async_remote_copy(
        src_ref=source, dst_ref=target, send_sem=sems.at[0, at], recv_sem=sems.at[1, there],
        device_id=device, device_id_type=MESH)


class Reduction:
    def __init__(self, here, grads, refs):
        self.here, self.grads = here, grads
        (self.half_out, self.half_in, self.plane_out, self.plane_in, self.depth_out, self.depth_in,
         self.final, self.gathered, self.half_sems, self.plane_sems, self.depth_sems, self.final_sems,
         self.gather_sems, self.pair_sems) = refs
        self.share = self.plane_out.shape[1]
        self.half = here.plane * self.share
        self.partner = here.device(core=1 - here.core)
        owners = [unit * here.depth // self.share for unit in range(self.share)]
        self.owned = [(unit, owner, unit - owners.index(owner)) for unit, owner in enumerate(owners)]

    @staticmethod
    def scratch(units, plane, depth):
        share = units // (CORES * plane)
        slots = -(-share // depth)
        unit = (ROWS, LANES)
        return [
            pltpu.VMEM((plane * share, *unit), LOW),
            pltpu.VMEM((plane * share, *unit), LOW),
            pltpu.VMEM((plane, share, *unit), LOW),
            pltpu.VMEM((plane, share, *unit), LOW),
            pltpu.VMEM((share, *unit), LOW),
            pltpu.VMEM((slots, depth, *unit), LOW),
            pltpu.VMEM((share, *unit), LOW),
            pltpu.VMEM((CORES, plane, share, *unit), LOW),
            pltpu.SemaphoreType.DMA((2, 1)),
            pltpu.SemaphoreType.DMA((2, plane)),
            pltpu.SemaphoreType.DMA((2, max(share, slots * depth))),
            pltpu.SemaphoreType.DMA((2, max(share, slots * depth))),
            pltpu.SemaphoreType.DMA((2, plane)),
            pltpu.SemaphoreType.DMA((2, plane)),
        ]

    def swap(self):
        return copy(self.half_out, self.half_in, self.half_sems, 0, 0, self.partner)

    def start_swap(self):
        self.half_out[...] = self.grads[pl.ds((1 - self.here.core) * self.half, self.half)].astype(LOW)
        self.swap().start()

    def to_plane(self, q, source_slot):
        here = self.here
        return copy(self.plane_out.at[q], self.plane_in.at[source_slot], self.plane_sems, q, source_slot, here.device(p=q))

    def start_plane(self):
        here = self.here
        self.swap().wait()
        mine = self.grads[pl.ds(here.core * self.half, self.half)]
        self.plane_out[...] = (mine + self.half_in[...].astype(WIDE)).astype(LOW).reshape(self.plane_out.shape)
        others(here.plane, here.p, lambda q: self.to_plane(q, here.p).start())

    def to_depth(self, unit, owner, slot, q):
        here = self.here
        return copy(self.depth_out.at[unit], self.depth_in.at[slot, q], self.depth_sems, unit,
                    slot * here.depth + q, here.device(z=owner))

    def start_depth(self):
        here = self.here
        self.plane_in[here.p] = self.plane_out[here.p]
        others(here.plane, here.p, lambda q: self.to_plane(q, q).wait())
        self.depth_out[...] = jnp.sum(self.plane_in[...].astype(WIDE), axis=0).astype(LOW)
        for unit, owner, slot in self.owned:
            @pl.when(here.z != owner)
            def _():
                self.to_depth(unit, owner, slot, here.z).start()

    def to_final(self, unit, slot, q):
        here = self.here
        return copy(self.final.at[unit], self.final.at[unit], self.final_sems, slot * here.depth + q, unit, here.device(z=q))

    def start_final(self):
        here = self.here
        for unit, owner, slot in self.owned:
            @pl.when(here.z == owner)
            def _():
                self.depth_in[slot, owner] = self.depth_out[unit]
                others(here.depth, here.z, lambda q: self.to_depth(unit, q, slot, q).wait_recv())
                self.final[unit] = jnp.sum(self.depth_in[slot].astype(WIDE), axis=0).astype(LOW)
                others(here.depth, here.z, lambda q: self.to_final(unit, slot, q).start())

    def to_gather(self, q, source_slot):
        here = self.here
        return copy(self.final, self.gathered.at[here.core, source_slot], self.gather_sems, q, source_slot, here.device(p=q))

    def to_pair(self, core, q):
        return copy(self.gathered.at[core, q], self.gathered.at[core, q], self.pair_sems, q, q, self.partner)

    def start_gather(self):
        here = self.here
        for unit, owner, slot in self.owned:
            @pl.when(here.z != owner)
            def _():
                self.to_depth(unit, owner, slot, here.z).wait_send()
                self.to_final(unit, slot, owner).wait_recv()

        others(here.plane, here.p, lambda q: self.to_gather(q, here.p).start())
        self.gathered[here.core, here.p] = self.final[...]
        self.to_pair(here.core, here.p).start()

    def pass_on(self):
        here = self.here

        def step(q):
            self.to_gather(q, q).wait_recv()
            self.to_pair(here.core, q).start()

        others(here.plane, here.p, step)

    def finish(self):
        here = self.here
        for unit, owner, slot in self.owned:
            @pl.when(here.z == owner)
            def _():
                others(here.depth, here.z, lambda q: self.to_final(unit, slot, q).wait_send())

        others(here.plane, here.p, lambda q: self.to_gather(q, q).wait_send())

        def arrived(q, carry):
            self.to_pair(1 - here.core, q).wait()
            return carry

        lax.fori_loop(0, here.plane, arrived, 0)
        return self.gathered[...].reshape(-1, ROWS, LANES)


class Halo:
    def __init__(self, here, sizes, step, sems, first, triples):
        self.items = []
        for index, (along_x, along_y, source, target) in enumerate(triples):
            sends = receives = None
            for along, place, size in ((along_x, here.sx, sizes[1]), (along_y, here.sy, sizes[2])):
                if not along:
                    continue
                ahead, behind = place < size - 1, place > 0
                send, receive = (ahead, behind) if step > 0 else (behind, ahead)
                sends = send if sends is None else jnp.logical_and(sends, send)
                receives = receive if receives is None else jnp.logical_and(receives, receive)
            device = (here.y, here.sx + step * along_x, here.sy + step * along_y)
            move = copy(source, target, sems, first + index, first + index, device)
            self.items.append((sends, receives, move, target))

    def start(self):
        for sends, _, move, _ in self.items:
            @pl.when(sends)
            def _():
                move.start()

    def wait(self):
        for _, receives, move, target in self.items:
            @pl.when(receives)
            def _():
                move.wait_recv()

            @pl.when(jnp.logical_not(receives))
            def _():
                target[...] = jnp.zeros(target.shape, target.dtype)

    def sent(self):
        for sends, _, move, _ in self.items:
            @pl.when(sends)
            def _():
                move.wait_send()


def kernel(sizes, volume, cotangent, w1, w2, w3, select, out1, out2, out3,
           vx, vy, vc, w1c, w2s, w3s, sel, local_sems, halo_sems, r1, r1_sems, s2, r2, r2_sems,
           dts, xoff, c1, g1, act1, act1s, lhs2, pre2, g2, g2y, g2x_in, g2y_in, g2c_in, lhs3, d3, d3x, d3y, d3c,
           lhs2t, c1t, d2s, d1, grads_a, grads_b, *reductions):
    here = Place(*sizes)
    _, size_x, size_y = sizes
    kept = cotangent.shape[0]

    loads = [
        pltpu.make_async_copy(select, sel, local_sems.at[0]),
        pltpu.make_async_copy(w2.at[:, :, pl.ds(1, 2)], w2s.at[:, :, pl.ds(0, 2)], local_sems.at[1]),
        pltpu.make_async_copy(w2.at[:, :, pl.ds(0, 1)], w2s.at[:, :, pl.ds(3, 1)], local_sems.at[2]),
        pltpu.make_async_copy(w3.at[:, :, pl.ds(1, 2)], w3s.at[:, :, pl.ds(0, 2)], local_sems.at[3]),
        pltpu.make_async_copy(w3.at[:, :, pl.ds(0, 1)], w3s.at[:, :, pl.ds(3, 1)], local_sems.at[4]),
    ]
    for load in loads:
        load.start()

    barrier = pltpu.get_barrier_semaphore()

    def greet(device):
        pl.semaphore_signal(barrier, inc=1, device_id=device, device_id_type=MESH)

    lower = jnp.logical_and(here.sx > 0, here.sy > 0)
    upper = jnp.logical_and(here.sx < size_x - 1, here.sy < size_y - 1)
    others(here.depth, here.z, lambda q: greet(here.device(z=q)))
    others(size_y, here.sy, lambda q: greet((here.y, here.sx, q)))
    others(here.plane, here.p, lambda q: greet(here.device(p=q)))

    @pl.when(lower)
    def _():
        greet((here.y, here.sx - 1, here.sy - 1))

    @pl.when(upper)
    def _():
        greet((here.y, here.sx + 1, here.sy + 1))

    pl.semaphore_wait(barrier, here.depth + size_y + here.plane - 3 + lower.astype(jnp.int32) + upper.astype(jnp.int32))

    volumes = Halo(here, sizes, 1, halo_sems, 0, ((1, 0, volume, vx), (0, 1, volume, vy), (1, 1, volume, vc)))
    volumes.start()

    def to_rows(q, source_slot):
        return copy(cotangent.at[:, q], r1.at[source_slot], r1_sems, q, source_slot, (here.y, q, here.sy))

    others(size_x, here.sx, lambda q: to_rows(q, here.sx).start())
    r1[here.sx] = cotangent[:, here.sx]

    w1c[...] = jnp.zeros(w1c.shape, WIDE)
    blank = jnp.zeros((4, 64), WIDE)
    for offset in range(5):
        base = offset * SLOT if offset < 3 else 128 + (offset - 3) * SLOT
        for dx in range(3):
            for dy in range(3):
                left = w1[dx, dy, offset].astype(WIDE) if offset <= 2 else blank
                right = w1[dx, dy, offset - 2].astype(WIDE) if offset >= 2 else blank
                w1c[pl.ds(base + (dx * 3 + dy) * 4, 4), :] = jnp.concatenate([left, right], axis=1)
    for ref in (w2s, w3s):
        ref[:, :, 2] = jnp.zeros((3, 3, *ref.shape[3:]), LOW)
    for index in range(8):
        dts[index, 0:8, :] = jnp.zeros((8, 128), WIDE)

    others(size_x, here.sx, lambda q: to_rows(q, q).wait())
    groups = size_x * kept
    spread = groups * ROWS
    lane = lax.broadcasted_iota(jnp.int32, (ROWS, spread), 1)
    row = lax.broadcasted_iota(jnp.int32, (ROWS, spread), 0)
    repeat = jnp.where((lane & (ROWS - 1)) == row, 1.0, 0.0).astype(LOW)
    wide = dot(r1[...].reshape(groups * size_y, ROWS), repeat).reshape(groups, size_y, spread)
    lane = lax.broadcasted_iota(jnp.int32, wide.shape, 2)
    group = lax.broadcasted_iota(jnp.int32, wide.shape, 0)
    strips = jnp.sum(jnp.where((lane >> 4) == group, wide, 0.0), axis=0)
    s2[...] = jnp.broadcast_to(strips[:, None, :], s2.shape)

    def to_cell(q, source_slot):
        return copy(s2.at[q], r2.at[source_slot], r2_sems, q, source_slot, (here.y, here.sx, q))

    others(size_y, here.sy, lambda q: to_cell(q, here.sy).start())
    r2[here.sy] = s2[here.sy]

    loads[0].wait()
    volumes.wait()

    for pair in range(8):
        before, inside = (vc, vx) if pair < 4 else (vy, volume)
        tiles = []
        for odd in range(2):
            x = (2 * pair + odd) % 8
            for channel in range(4):
                tiles += [before[channel, x].astype(WIDE), inside[channel, x].astype(WIDE)]
        dts[pair, 8:136, :] = jnp.concatenate(tiles, axis=0).T
    for offset in range(5):
        for pair in range(8):
            xoff[offset, pair * 32:(pair + 1) * 32, :] = dts[pair, pl.ds(7 + offset, 32, stride=4), :].astype(LOW)
    for part, offsets in enumerate(((0, 1, 2), (3, 4))):
        blocks = []
        for offset in offsets:
            blocks += [xoff[offset, 32:256, :], xoff[offset, 0:224, :]]
        chosen = dot(jnp.concatenate(blocks, axis=1), sel[0:256 * len(offsets), :])
        for cell in range(7):
            c1[cell, :, part * 128:(part + 1) * 128] = chosen[:, cell * 128:(cell + 1) * 128].astype(LOW)
    first = w1c[...].astype(LOW)
    for cell in range(7):
        pre = dot(c1[cell], first)
        if cell >= 3:
            g1[cell - 3] = gelu_slope(pre[96:224])
        act = gelu(pre)
        act1[cell] = act.astype(LOW)
        act1s[cell] = down(act, 32).astype(LOW)

    for index, (x, y) in enumerate(CELLS):
        for dx in range(3):
            for dy in range(3):
                at = (dx * 3 + dy) * 256
                rows = slice((2 * x + dx) * 32, (2 * x + dx + 1) * 32)
                lhs2[index * 32:(index + 1) * 32, at:at + 128] = act1[2 * y + dy, rows, :]
                lhs2[index * 32:(index + 1) * 32, at + 128:at + 256] = act1s[2 * y + dy, rows, :]
    for load in loads[1:3]:
        load.wait()
    second = w2s[...].reshape(2304, 64)
    pre2[...] = dot(lhs2[...], second)
    for index, (x, y) in enumerate(CELLS):
        pre = jnp.concatenate(
            [pre2[pl.ds(index * 32 + parity, 16, stride=2), :] for parity in range(2)], axis=1)
        if index < 4:
            slope = gelu_slope(pre)
            g2[index] = slope
            if index in (0, 2):
                g2y[index // 2] = slope
        act = gelu(pre)
        at = (x * 3 + y) * 256
        lhs3[:, at:at + 128] = act
        lhs3[:, at + 128:at + 256] = down(act, 16)
    slopes = Halo(here, sizes, -1, halo_sems, 3, (
        (1, 0, g2.at[pl.ds(0, 2)], g2x_in), (0, 1, g2y, g2y_in), (1, 1, g2.at[pl.ds(0, 1)], g2c_in)))
    slopes.start()

    others(size_y, here.sy, lambda q: to_cell(q, q).wait())
    strips = jnp.max(r2[...], axis=1).T.astype(LOW)
    channel = lax.broadcasted_iota(jnp.int32, (size_y, 256), 1)
    owner = lax.broadcasted_iota(jnp.int32, (size_y, 256), 0)
    choose = jnp.where(lax.rem(channel // kept, size_y) == owner, 1.0, 0.0).astype(LOW)
    wide = dot(strips, choose).reshape(groups, ROWS, 256)
    channel = lax.broadcasted_iota(jnp.int32, wide.shape, 2)
    group = lax.broadcasted_iota(jnp.int32, wide.shape, 0)
    mine = (channel // (kept * size_y)) * kept + lax.rem(channel, kept) == group
    upstream = jnp.sum(jnp.where(mine, wide, 0.0), axis=0)
    for load in loads[3:5]:
        load.wait()
    third = w3s[...].reshape(2304, 256)
    pre = dot(lhs3[...].astype(LOW), third)
    delta = (gelu_slope(pre) * upstream).astype(LOW)
    d3[...] = delta
    deltas = Halo(here, sizes, -1, halo_sems, 6, ((1, 0, d3, d3x), (0, 1, d3, d3y), (1, 1, d3, d3c)))
    deltas.start()

    for tap in range(9):
        turned = lhs3[:, tap * 256:(tap + 1) * 256].T.astype(LOW)
        grad = dot(turned, delta)
        for dz, rows in enumerate((192, 0, 64)):
            for lanes in range(2):
                at = lanes * 108 + (tap * 3 + dz) * 4
                grads_a[at:at + 4] = grad[rows:rows + 64, lanes * 128:(lanes + 1) * 128].reshape(4, ROWS, LANES)
    spare = grads_a.shape[0] - THIRD_UNITS
    if spare:
        grads_a[THIRD_UNITS:] = jnp.zeros((spare, ROWS, LANES), WIDE)
    many = len(reductions) // 2
    large = Reduction(here, grads_a, reductions[:many])
    small = Reduction(here, grads_b, reductions[many:])
    large.start_swap()

    for block in range(18):
        lhs2t[block * 128:(block + 1) * 128, :] = lhs2[0:128, block * 128:(block + 1) * 128].astype(WIDE).T.astype(LOW)
    for cell in range(4):
        for half in range(2):
            lanes = slice(half * 128, (half + 1) * 128)
            c1t[lanes, cell * 128:(cell + 1) * 128] = c1[3 + cell, 96:224, lanes].astype(WIDE).T.astype(LOW)

    large.start_plane()
    slopes.wait()
    deltas.wait()

    sources = {(0, 0): 0, (1, 0): 1, (0, 1): 2, (1, 1): 3}
    back = dot(jnp.concatenate([d3[...], d3x[...], d3y[...], d3c[...]], axis=0), third, transposed=True)
    reads = {0: ((0, 1),), 1: ((0, 2), (1, 0)), 2: ((1, 1),)}
    slope_at = {(0, 0): g2.at[0], (0, 1): g2.at[1], (1, 0): g2.at[2], (1, 1): g2.at[3],
                (2, 0): g2x_in.at[0], (2, 1): g2x_in.at[1], (0, 2): g2y_in.at[0], (1, 2): g2y_in.at[1],
                (2, 2): g2c_in.at[0]}
    for a in range(3):
        for b in range(3):
            total = 0.0
            for from_x, dx in reads[a]:
                for from_y, dy in reads[b]:
                    at, tap = sources[from_x, from_y] * 16, (dx * 3 + dy) * 256
                    total = total + back[at:at + 16, tap:tap + 256]
            value = slope_at[a, b][...] * (total[:, 0:128] + up(total[:, 128:256]))
            d2s[a * 3 + b, pl.ds(0, 16, stride=2), :] = value[:, 0:64]
            d2s[a * 3 + b, pl.ds(1, 16, stride=2), :] = value[:, 64:128]

    delta = jnp.concatenate([d2s[a * 3 + b].astype(LOW) for a, b in OWN], axis=0)
    grad = dot(lhs2t[...], delta)

    def second_block(block):
        if block > 26:
            return jnp.zeros((64, 64), WIDE)
        start = (block // 3) * 256 + (192, 0, 64)[block % 3]
        return grad[start:start + 64]

    for block in range(14):
        both = jnp.concatenate([second_block(block), second_block(block + 14)], axis=1)
        grads_b[block * 4:(block + 1) * 4] = both.reshape(4, ROWS, LANES)

    sums = {}
    for dx in range(3):
        for dy in range(3):
            cells = [((1 if dx == 0 else 0) + a, (1 if dy == 0 else 0) + b) for a, b in OWN]
            stacked = jnp.concatenate([d2s[a * 3 + b].astype(LOW) for a, b in cells], axis=0)
            tap = (dx * 3 + dy) * 256
            back = dot(stacked, second[tap:tap + 256], transposed=True)
            for index, (a, b) in enumerate(cells):
                place = (2 * a + dx - 1, 2 * b + dy - 1)
                part = back[index * 32:(index + 1) * 32]
                sums[place] = sums[place] + part if place in sums else part
    for a in range(4):
        for b in range(4):
            total = sums[a, b]
            value = g1[b, a * 32:(a + 1) * 32] * (total[:, 0:128] + up(total[:, 128:256]))
            d1[b * 128 + a * 32:b * 128 + (a + 1) * 32, :] = value.astype(LOW)
    grad = dot(c1t[...], d1[...])
    for dz in range(3):
        start = (0, SLOT, 2 * SLOT)[dz]
        other = (2 * SLOT, 128, 128 + SLOT)[dz]
        w1c[dz * SLOT:(dz + 1) * SLOT, :] = jnp.concatenate(
            [grad[start:start + SLOT, 0:64] + grad[other:other + SLOT, 64:128], jnp.zeros((SLOT, 64), WIDE)], axis=1)
    w1c[120:128, :] = jnp.zeros((8, 128), WIDE)
    grads_b[SECOND_UNITS:SECOND_UNITS + FIRST_UNITS] = w1c[0:128, :].reshape(FIRST_UNITS, ROWS, LANES)

    small.start_swap()
    large.start_depth()
    small.start_plane()
    large.start_final()
    small.start_depth()
    large.start_gather()
    small.start_final()
    large.pass_on()
    small.start_gather()
    small.pass_on()
    total = large.finish()
    for lanes in range(2):
        out3[:, lanes * 128:(lanes + 1) * 128] = total[lanes * 108:(lanes + 1) * 108].reshape(1728, LANES)
    total = small.finish()
    both = total[0:SECOND_UNITS].reshape(896, LANES)
    out2[0:896, :] = both[:, 0:64]
    out2[896:1728, :] = both[0:832, 64:128]
    w1c[0:128, :] = total[SECOND_UNITS:SECOND_UNITS + FIRST_UNITS].reshape(128, LANES).astype(WIDE)
    for dx in range(3):
        for dy in range(3):
            for dz in range(3):
                out1[dx, dy, dz] = w1c[pl.ds(dz * SLOT + (dx * 3 + dy) * 4, 4), 0:64]
    volumes.sent()
    slopes.sent()
    deltas.sent()


def local(sizes, volume, cotangent, first_weight, second_weight, third_weight):
    dp, size_x, size_y = sizes
    plane = min(4, size_y // CORES) * dp
    depth = size_x * (size_y // (CORES * min(4, size_y // CORES)))
    grain = CORES * plane
    units_a = -(-THIRD_UNITS // grain) * grain
    units_b = -(-(FIRST_UNITS + SECOND_UNITS) // grain) * grain
    kept = cotangent.shape[1]
    spread = size_x * kept * ROWS
    vmem, sems = pltpu.VMEM, pltpu.SemaphoreType.DMA
    block = volume.shape[1:]
    whole, anywhere = pl.BlockSpec(memory_space=pltpu.VMEM), pl.BlockSpec(memory_space=pl.ANY)
    grads = pl.pallas_call(
        functools.partial(kernel, sizes),
        out_shape=(
            jax.ShapeDtypeStruct((3, 3, 3, 4, 64), WIDE),
            jax.ShapeDtypeStruct((1728, 64), LOW),
            jax.ShapeDtypeStruct((1728, 256), LOW),
        ),
        in_specs=[whole, whole, whole, anywhere, anywhere, anywhere],
        out_specs=(whole, whole, whole),
        scratch_shapes=[
            vmem(block, LOW), vmem(block, LOW), vmem(block, LOW),
            vmem((256, 128), WIDE), vmem((3, 3, 4, 64, 64), LOW), vmem((3, 3, 4, 64, 256), LOW), vmem((768, 896), LOW),
            sems((5,)), sems((2, 9)),
            vmem((size_x, kept, size_y, ROWS), LOW), sems((2, size_x)),
            vmem((size_y, 8, spread), WIDE), vmem((size_y, 8, spread), WIDE), sems((2, size_y)),
            vmem((8, 136, 128), WIDE), vmem((5, 256, 128), LOW), vmem((7, 224, 256), LOW), vmem((4, 128, 128), WIDE),
            vmem((7, 224, 128), LOW), vmem((7, 224, 128), LOW), vmem((288, 2304), LOW), vmem((288, 64), WIDE),
            vmem((4, 16, 128), WIDE), vmem((2, 16, 128), WIDE),
            vmem((2, 16, 128), WIDE), vmem((2, 16, 128), WIDE), vmem((1, 16, 128), WIDE),
            vmem((16, 2304), WIDE), vmem((16, 256), LOW), vmem((16, 256), LOW), vmem((16, 256), LOW), vmem((16, 256), LOW),
            vmem((2304, 128), LOW), vmem((256, 512), LOW), vmem((9, 32, 64), WIDE), vmem((512, 128), LOW),
            vmem((units_a, ROWS, LANES), WIDE), vmem((units_b, ROWS, LANES), WIDE),
            *Reduction.scratch(units_a, plane, depth), *Reduction.scratch(units_b, plane, depth),
        ],
        compiler_params=pltpu.CompilerParams(collective_id=1, has_side_effects=True, vmem_limit_bytes=48 * 2**20),
        cost_estimate=pl.CostEstimate(flops=1_000_000_000, bytes_accessed=8_000_000, transcendentals=1_000_000),
    )(volume[0], cotangent[0], first_weight, second_weight, third_weight, jnp.asarray(selection(), LOW))
    return (
        grads[0],
        grads[1].astype(WIDE).reshape(3, 3, 3, 64, 64),
        grads[2].astype(WIDE).reshape(3, 3, 3, 64, 256),
    )


def solution(mesh):
    sizes = tuple(mesh.shape[name] for name in ("dp", "sx", "sy"))
    placed = (P("dp", None, "sx", "sy", None), P("dp", ("sx", "sy"), None, None, None), P(), P(), P())
    return jax.shard_map(
        functools.partial(local, sizes), mesh=mesh, in_specs=placed, out_specs=(P(), P(), P()), check_vma=False)
```

```python
import functools

import jax
import jax.numpy as jnp
import numpy as np
from jax import lax
from jax.experimental import pallas as pl
from jax.experimental.pallas import tpu as pltpu
from jax.sharding import PartitionSpec as P

MESH = pl.DeviceIdType.MESH
LOW, WIDE = jnp.bfloat16, jnp.float32
CORES = 2
ROWS, LANES = 16, 128
SLOT = 40
FIRST_UNITS, SECOND_UNITS, THIRD_UNITS = 8, 56, 216
OWN = ((0, 0), (0, 1), (1, 0), (1, 1))
CELLS = [(1 + a, 1 + b) for a, b in OWN] + [(0, 0), (0, 1), (0, 2), (1, 0), (2, 0)]


def selection():
    result = np.zeros((3, 2, 2, 4, 16, 7, LANES), np.float32)
    for offset in range(3):
        for dx, (pair, odd) in enumerate(((1, 1), (0, 0), (0, 1))):
            for channel in range(4):
                for cell in range(7):
                    for dy in range(3):
                        lane = offset * SLOT + (dx * 3 + dy) * 4 + channel
                        result[offset, pair, odd, channel, 2 * cell + dy + 1, cell, lane] = 1
    return result.reshape(768, 7 * LANES)


def gelu_parts(v):
    square = v * v
    t = jnp.tanh(np.sqrt(2 / np.pi) * (v + 0.044715 * (v * square)))
    return t, square


def gelu(v):
    t, _ = gelu_parts(v)
    return 0.5 * v * (1 + t)


def gelu_slope(v):
    t, square = gelu_parts(v)
    return 0.5 * (1 + t) + 0.5 * v * (1 - t * t) * (np.sqrt(2 / np.pi) * (1 + 3 * 0.044715 * square))


def dot(a, b, transposed=False):
    return lax.dot_general(a, b, (((1,), (1 if transposed else 0,)), ((), ())), preferred_element_type=WIDE)


def down(v, period):
    row = lax.broadcasted_iota(jnp.int32, v.shape, 0)
    return jnp.where((row & (period - 1)) == 0, 0.0, pltpu.roll(v, 1, axis=0))


def up(v):
    row = lax.broadcasted_iota(jnp.int32, v.shape, 0)
    return jnp.where(row == v.shape[0] - 1, 0.0, pltpu.roll(v, v.shape[0] - 1, axis=0))


class Place:
    def __init__(self, dp, sx, sy):
        self.chips_x = min(4, sy // CORES)
        self.low_z, self.chips_y = sx, dp
        self.plane = self.chips_x * dp
        self.depth = sx * (sy // (CORES * self.chips_x))
        self.y, self.sx, self.sy = (lax.axis_index(name) for name in ("dp", "sx", "sy"))
        self.core = lax.rem(self.sy, CORES)
        self.p = lax.rem(self.sy // CORES, self.chips_x) * dp + self.y
        self.mixed = CORES * self.chips_x
        self.t = lax.rem(self.sy, self.mixed)
        self.z = (self.sy // self.mixed) * sx + self.sx

    def device(self, core=None, p=None, z=None):
        core = self.core if core is None else core
        p = self.p if p is None else p
        z = self.z if z is None else z
        chip_x, y = p // self.chips_y, lax.rem(p, self.chips_y)
        high, low = z // self.low_z, lax.rem(z, self.low_z)
        return (y, low, (high * self.chips_x + chip_x) * CORES + core)


def others(count, me, body):
    def step(distance, carry):
        body(lax.rem(me + distance, count))
        return carry

    lax.fori_loop(1, count, step, 0)


def copy(source, target, sems, at, there, device):
    return pltpu.make_async_remote_copy(
        src_ref=source, dst_ref=target, send_sem=sems.at[0, at], recv_sem=sems.at[1, there],
        device_id=device, device_id_type=MESH)


class Reduction:
    def __init__(self, here, grads, refs, direct):
        self.here, self.grads, self.direct = here, grads, direct
        (self.half_out, self.half_in, self.plane_out, self.plane_in, self.depth_out, self.depth_in,
         self.final, self.gathered, self.half_sems, self.plane_sems, self.depth_sems, self.final_sems,
         self.gather_sems, self.pair_sems) = refs
        self.share = self.plane_out.shape[1]
        self.half = here.plane * self.share
        self.partner = here.device(core=1 - here.core)
        owners = [unit * here.depth // self.share for unit in range(self.share)]
        self.owned = [] if direct else [(unit, owner, unit - owners.index(owner)) for unit, owner in enumerate(owners)]

    @staticmethod
    def scratch(units, plane, depth, direct):
        share = units // (CORES * plane)
        slots = share if direct else -(-share // depth)
        unit = (ROWS, LANES)
        return [
            pltpu.VMEM((plane * share, *unit), LOW),
            pltpu.VMEM((plane * share, *unit), LOW),
            pltpu.VMEM((plane, share, *unit), LOW),
            pltpu.VMEM((plane, share, *unit), LOW),
            pltpu.VMEM((share, *unit), LOW),
            pltpu.VMEM((depth, slots, *unit) if direct else (slots, depth, *unit), LOW),
            pltpu.VMEM((share, *unit), LOW),
            pltpu.VMEM((CORES, plane, share, *unit), LOW),
            pltpu.SemaphoreType.DMA((2, 1)),
            pltpu.SemaphoreType.DMA((2, plane)),
            pltpu.SemaphoreType.DMA((2, max(share, slots * depth))),
            pltpu.SemaphoreType.DMA((2, max(share, slots * depth))),
            pltpu.SemaphoreType.DMA((2, plane)),
            pltpu.SemaphoreType.DMA((2, plane)),
        ]

    def swap(self):
        return copy(self.half_out, self.half_in, self.half_sems, 0, 0, self.partner)

    def start_swap(self):
        self.half_out[...] = self.grads[pl.ds((1 - self.here.core) * self.half, self.half)].astype(LOW)
        self.swap().start()

    def to_plane(self, q, source_slot):
        here = self.here
        return copy(self.plane_out.at[q], self.plane_in.at[source_slot], self.plane_sems, q, source_slot, here.device(p=q))

    def start_plane(self):
        here = self.here
        self.swap().wait()
        mine = self.grads[pl.ds(here.core * self.half, self.half)]
        self.plane_out[...] = (mine + self.half_in[...].astype(WIDE)).astype(LOW).reshape(self.plane_out.shape)
        others(here.plane, here.p, lambda q: self.to_plane(q, here.p).start())

    def to_depth(self, unit, owner, slot, q):
        here = self.here
        return copy(self.depth_out.at[unit], self.depth_in.at[slot, q], self.depth_sems, unit,
                    slot * here.depth + q, here.device(z=owner))

    def start_depth(self):
        here = self.here
        self.plane_in[here.p] = self.plane_out[here.p]
        others(here.plane, here.p, lambda q: self.to_plane(q, q).wait())
        self.depth_out[...] = jnp.sum(self.plane_in[...].astype(WIDE), axis=0).astype(LOW)
        if self.direct:
            others(here.depth, here.z, lambda q: self.to_all(q, here.z).start())
            return
        for unit, owner, slot in self.owned:
            @pl.when(here.z != owner)
            def _():
                self.to_depth(unit, owner, slot, here.z).start()

    def to_all(self, q, source_slot):
        here = self.here
        return copy(self.depth_out, self.depth_in.at[source_slot], self.depth_sems, q, source_slot, here.device(z=q))

    def to_final(self, unit, slot, q):
        here = self.here
        return copy(self.final.at[unit], self.final.at[unit], self.final_sems, slot * here.depth + q, unit, here.device(z=q))

    def start_final(self):
        here = self.here
        for unit, owner, slot in self.owned:
            @pl.when(here.z == owner)
            def _():
                self.depth_in[slot, owner] = self.depth_out[unit]
                others(here.depth, here.z, lambda q: self.to_depth(unit, q, slot, q).wait_recv())
                self.final[unit] = jnp.sum(self.depth_in[slot].astype(WIDE), axis=0).astype(LOW)
                others(here.depth, here.z, lambda q: self.to_final(unit, slot, q).start())

    def to_gather(self, q, source_slot):
        here = self.here
        return copy(self.final, self.gathered.at[here.core, source_slot], self.gather_sems, q, source_slot, here.device(p=q))

    def to_pair(self, core, q):
        return copy(self.gathered.at[core, q], self.gathered.at[core, q], self.pair_sems, q, q, self.partner)

    def start_gather(self):
        here = self.here
        if self.direct:
            self.depth_in[here.z] = self.depth_out[...]
            others(here.depth, here.z, lambda q: self.to_all(q, q).wait())
            self.final[...] = jnp.sum(self.depth_in[...].astype(WIDE), axis=0).astype(LOW)
        for unit, owner, slot in self.owned:
            @pl.when(here.z != owner)
            def _():
                self.to_depth(unit, owner, slot, here.z).wait_send()
                self.to_final(unit, slot, owner).wait_recv()

        others(here.plane, here.p, lambda q: self.to_gather(q, here.p).start())
        self.gathered[here.core, here.p] = self.final[...]
        self.to_pair(here.core, here.p).start()

    def pass_on(self):
        here = self.here

        def step(q):
            self.to_gather(q, q).wait_recv()
            self.to_pair(here.core, q).start()

        others(here.plane, here.p, step)

    def finish(self):
        here = self.here
        for unit, owner, slot in self.owned:
            @pl.when(here.z == owner)
            def _():
                others(here.depth, here.z, lambda q: self.to_final(unit, slot, q).wait_send())

        others(here.plane, here.p, lambda q: self.to_gather(q, q).wait_send())

        def arrived(q, carry):
            self.to_pair(1 - here.core, q).wait()
            return carry

        lax.fori_loop(0, here.plane, arrived, 0)
        return self.gathered[...].reshape(-1, ROWS, LANES)


class Halo:
    def __init__(self, here, sizes, step, sems, first, triples):
        self.items = []
        for index, (along_x, along_y, source, target) in enumerate(triples):
            sends = receives = None
            for along, place, size in ((along_x, here.sx, sizes[1]), (along_y, here.sy, sizes[2])):
                if not along:
                    continue
                ahead, behind = place < size - 1, place > 0
                send, receive = (ahead, behind) if step > 0 else (behind, ahead)
                sends = send if sends is None else jnp.logical_and(sends, send)
                receives = receive if receives is None else jnp.logical_and(receives, receive)
            device = (here.y, here.sx + step * along_x, here.sy + step * along_y)
            move = copy(source, target, sems, first + index, first + index, device)
            self.items.append((sends, receives, move, target))

    def start(self):
        for sends, _, move, _ in self.items:
            @pl.when(sends)
            def _():
                move.start()

    def wait(self):
        for _, receives, move, target in self.items:
            @pl.when(receives)
            def _():
                move.wait_recv()

            @pl.when(jnp.logical_not(receives))
            def _():
                target[...] = jnp.zeros(target.shape, target.dtype)

    def sent(self):
        for sends, _, move, _ in self.items:
            @pl.when(sends)
            def _():
                move.wait_send()


def kernel(sizes, volume_hbm, cotangent_hbm, w1_hbm, w2, w3, select, out1, out2, out3,
           volume, vx, vy, vc, cotangent, w1, w1c, w2s, w3s, sel, local_sems, halo_sems, s1, r1, r1_sems, s2, r2, r2_sems,
           dts, xoff, c1, g1, act1, act1s, lhs2, pre2, g2, g2y, g2x_in, g2y_in, g2c_in, lhs3, d3, d3x, d3y, d3c,
           lhs2t, c1t, d2s, d1, grads_a, grads_b, *reductions):
    here = Place(*sizes)
    _, size_x, size_y = sizes
    mixed, depth = here.mixed, here.depth
    kept, high = cotangent.shape[0], size_y // mixed

    barrier = pltpu.get_barrier_semaphore()

    def greet(device):
        pl.semaphore_signal(barrier, inc=1, device_id=device, device_id_type=MESH)

    def at_mixed(t):
        return (here.y, here.sx, here.sy - here.t + t)

    others(depth, here.z, lambda q: greet(here.device(z=q)))
    others(mixed, here.t, lambda q: greet(at_mixed(q)))
    others(here.plane, here.p, lambda q: greet(here.device(p=q)))
    expected = depth + mixed + here.plane - 3
    for along_x in range(2):
        for step in (-1, 1):
            inside = here.sy > 0 if step < 0 else here.sy < size_y - 1
            if along_x:
                inside = jnp.logical_and(inside, here.sx > 0 if step < 0 else here.sx < size_x - 1)
            expected = expected + inside.astype(jnp.int32)

            @pl.when(inside)
            def _():
                greet((here.y, here.sx + step * along_x, here.sy + step))

    loads = [
        pltpu.make_async_copy(w1_hbm, w1, local_sems.at[0]),
        pltpu.make_async_copy(cotangent_hbm, cotangent, local_sems.at[1]),
        pltpu.make_async_copy(volume_hbm, volume, local_sems.at[2]),
        pltpu.make_async_copy(select, sel, local_sems.at[3]),
        pltpu.make_async_copy(w2.at[:, :, pl.ds(1, 2)], w2s.at[:, :, pl.ds(0, 2)], local_sems.at[4]),
        pltpu.make_async_copy(w2.at[:, :, pl.ds(0, 1)], w2s.at[:, :, pl.ds(3, 1)], local_sems.at[5]),
        pltpu.make_async_copy(w3.at[:, :, pl.ds(1, 2)], w3s.at[:, :, pl.ds(0, 2)], local_sems.at[6]),
        pltpu.make_async_copy(w3.at[:, :, pl.ds(0, 1)], w3s.at[:, :, pl.ds(3, 1)], local_sems.at[7]),
    ]
    for load in loads:
        load.start()
    for ref in (w2s, w3s):
        ref[:, :, 2] = jnp.zeros((3, 3, *ref.shape[3:]), LOW)
    for index in range(8):
        dts[index, 0:8, :] = jnp.zeros((8, 128), WIDE)
    w1c[...] = jnp.zeros(w1c.shape, WIDE)
    blank = jnp.zeros((4, 64), WIDE)

    loads[0].wait()
    for offset in range(5):
        base = offset * SLOT if offset < 3 else 128 + (offset - 3) * SLOT
        for dx in range(3):
            for dy in range(3):
                left = w1[dx, dy, offset].astype(WIDE) if offset <= 2 else blank
                right = w1[dx, dy, offset - 2].astype(WIDE) if offset >= 2 else blank
                w1c[pl.ds(base + (dx * 3 + dy) * 4, 4), :] = jnp.concatenate([left, right], axis=1)

    loads[1].wait()
    spread = size_x * kept * ROWS
    lane = lax.broadcasted_iota(jnp.int32, (ROWS, spread), 1)
    row = lax.broadcasted_iota(jnp.int32, (ROWS, spread), 0)
    repeat = jnp.where((lane & (ROWS - 1)) == row, 1.0, 0.0).astype(LOW)
    wide = dot(cotangent[...].reshape(kept * size_x * size_y, ROWS), repeat).reshape(kept * size_x, size_y, spread)
    lane = lax.broadcasted_iota(jnp.int32, wide.shape, 2)
    group = lax.broadcasted_iota(jnp.int32, wide.shape, 0)
    strips = jnp.sum(jnp.where((lane >> 4) == lax.rem(group, size_x) * kept + group // size_x, wide, 0.0), axis=0)
    rows = 8 // high
    for t in range(mixed):
        for part in range(high):
            y = part * mixed + t
            s1[t, part * rows:(part + 1) * rows, :] = jnp.broadcast_to(strips[y:y + 1, :], (rows, spread))

    pl.semaphore_wait(barrier, expected)
    volumes = Halo(here, sizes, 1, halo_sems, 0, (
        (1, 0, volume_hbm, vx), (0, 1, volume_hbm, vy), (1, 1, volume_hbm, vc)))
    volumes.start()

    def to_mixed(q, source_slot):
        return copy(s1.at[q], r1.at[source_slot], r1_sems, q, source_slot, at_mixed(q))

    def to_cell(q, source_slot):
        return copy(s2.at[q], r2.at[source_slot], r2_sems, q, source_slot, here.device(z=q))

    others(mixed, here.t, lambda q: to_mixed(q, here.t).start())
    r1[here.t] = s1[here.t]
    others(mixed, here.t, lambda q: to_mixed(q, q).wait())
    for part in range(high):
        strips = jnp.max(r1[:, part * rows:(part + 1) * rows, :], axis=1)
        for x in range(size_x):
            s2[part * size_x + x] = strips[:, x * kept * ROWS:(x + 1) * kept * ROWS]
    others(depth, here.z, lambda q: to_cell(q, here.z).start())
    r2[here.z] = s2[here.z]

    for load in loads[2:4]:
        load.wait()
    volumes.wait()

    for pair in range(8):
        before, inside = (vc, vx) if pair < 4 else (vy, volume)
        tiles = []
        for channel in range(4):
            at = channel * 64 + (pair % 4) * 16
            tiles.append([ref[at:at + 16, :].astype(WIDE) for ref in (before, inside)])
        ordered = [both[odd * 8:(odd + 1) * 8] for odd in range(2) for refs in tiles for both in refs]
        dts[pair, 8:136, :] = jnp.concatenate(ordered, axis=0).T
    for offset in range(5):
        for pair in range(8):
            xoff[offset, pair * 32:(pair + 1) * 32, :] = dts[pair, pl.ds(7 + offset, 32, stride=4), :].astype(LOW)
    for part, offsets in enumerate(((0, 1, 2), (3, 4))):
        blocks = []
        for offset in offsets:
            blocks += [xoff[offset, 32:256, :], xoff[offset, 0:224, :]]
        chosen = dot(jnp.concatenate(blocks, axis=1), sel[0:256 * len(offsets), :])
        for cell in range(7):
            c1[cell, :, part * 128:(part + 1) * 128] = chosen[:, cell * 128:(cell + 1) * 128].astype(LOW)
    first = w1c[...].astype(LOW)
    for cell in range(7):
        pre = dot(c1[cell], first)
        if cell >= 3:
            g1[cell - 3] = gelu_slope(pre[96:224])
        act = gelu(pre)
        act1[cell] = act.astype(LOW)
        act1s[cell] = down(act, 32).astype(LOW)

    for index, (x, y) in enumerate(CELLS):
        for dx in range(3):
            for dy in range(3):
                at = (dx * 3 + dy) * 256
                rows = slice((2 * x + dx) * 32, (2 * x + dx + 1) * 32)
                lhs2[index * 32:(index + 1) * 32, at:at + 128] = act1[2 * y + dy, rows, :]
                lhs2[index * 32:(index + 1) * 32, at + 128:at + 256] = act1s[2 * y + dy, rows, :]
    for load in loads[4:6]:
        load.wait()
    second = w2s[...].reshape(2304, 64)
    pre2[...] = dot(lhs2[...], second)
    for index, (x, y) in enumerate(CELLS):
        pre = jnp.concatenate(
            [pre2[pl.ds(index * 32 + parity, 16, stride=2), :] for parity in range(2)], axis=1)
        if index < 4:
            slope = gelu_slope(pre)
            g2[index] = slope
            if index in (0, 2):
                g2y[index // 2] = slope
        act = gelu(pre)
        at = (x * 3 + y) * 256
        lhs3[:, at:at + 128] = act
        lhs3[:, at + 128:at + 256] = down(act, 16)
    slopes = Halo(here, sizes, -1, halo_sems, 3, (
        (1, 0, g2.at[pl.ds(0, 2)], g2x_in), (0, 1, g2y, g2y_in), (1, 1, g2.at[pl.ds(0, 1)], g2c_in)))
    slopes.start()

    others(depth, here.z, lambda q: to_cell(q, q).wait())
    strips = r2[...].reshape(depth * mixed, kept * ROWS).T.astype(LOW)
    sender = lax.broadcasted_iota(jnp.int32, (depth * mixed, 256), 0)
    channel = lax.broadcasted_iota(jnp.int32, (depth * mixed, 256), 1)
    z, t = sender // mixed, lax.rem(sender, mixed)
    channel = channel - ((lax.rem(z, size_x) * size_y + (z // size_x) * mixed + t) * kept)
    upstream = 0.0
    for k in range(kept):
        choose = jnp.where(channel == k, 1.0, 0.0).astype(LOW)
        upstream = upstream + dot(strips[k * ROWS:(k + 1) * ROWS], choose)
    for load in loads[6:8]:
        load.wait()
    third = w3s[...].reshape(2304, 256)
    pre = dot(lhs3[...].astype(LOW), third)
    delta = (gelu_slope(pre) * upstream).astype(LOW)
    d3[...] = delta
    deltas = Halo(here, sizes, -1, halo_sems, 6, ((1, 0, d3, d3x), (0, 1, d3, d3y), (1, 1, d3, d3c)))
    deltas.start()

    for tap in range(9):
        turned = lhs3[:, tap * 256:(tap + 1) * 256].T.astype(LOW)
        grad = dot(turned, delta)
        for dz, rows in enumerate((192, 0, 64)):
            for lanes in range(2):
                at = lanes * 108 + (tap * 3 + dz) * 4
                grads_a[at:at + 4] = grad[rows:rows + 64, lanes * 128:(lanes + 1) * 128].reshape(4, ROWS, LANES)
    spare = grads_a.shape[0] - THIRD_UNITS
    if spare:
        grads_a[THIRD_UNITS:] = jnp.zeros((spare, ROWS, LANES), WIDE)
    many = len(reductions) // 2
    large = Reduction(here, grads_a, reductions[:many], False)
    small = Reduction(here, grads_b, reductions[many:], True)
    large.start_swap()

    for block in range(18):
        lhs2t[block * 128:(block + 1) * 128, :] = lhs2[0:128, block * 128:(block + 1) * 128].astype(WIDE).T.astype(LOW)
    for cell in range(4):
        for half in range(2):
            lanes = slice(half * 128, (half + 1) * 128)
            c1t[lanes, cell * 128:(cell + 1) * 128] = c1[3 + cell, 96:224, lanes].astype(WIDE).T.astype(LOW)

    large.start_plane()
    slopes.wait()
    deltas.wait()

    sources = {(0, 0): 0, (1, 0): 1, (0, 1): 2, (1, 1): 3}
    back = dot(jnp.concatenate([d3[...], d3x[...], d3y[...], d3c[...]], axis=0), third, transposed=True)
    reads = {0: ((0, 1),), 1: ((0, 2), (1, 0)), 2: ((1, 1),)}
    slope_at = {(0, 0): g2.at[0], (0, 1): g2.at[1], (1, 0): g2.at[2], (1, 1): g2.at[3],
                (2, 0): g2x_in.at[0], (2, 1): g2x_in.at[1], (0, 2): g2y_in.at[0], (1, 2): g2y_in.at[1],
                (2, 2): g2c_in.at[0]}
    for a in range(3):
        for b in range(3):
            total = 0.0
            for from_x, dx in reads[a]:
                for from_y, dy in reads[b]:
                    at, tap = sources[from_x, from_y] * 16, (dx * 3 + dy) * 256
                    total = total + back[at:at + 16, tap:tap + 256]
            value = slope_at[a, b][...] * (total[:, 0:128] + up(total[:, 128:256]))
            d2s[a * 3 + b, pl.ds(0, 16, stride=2), :] = value[:, 0:64]
            d2s[a * 3 + b, pl.ds(1, 16, stride=2), :] = value[:, 64:128]

    delta = jnp.concatenate([d2s[a * 3 + b].astype(LOW) for a, b in OWN], axis=0)
    grad = dot(lhs2t[...], delta)

    def second_block(block):
        if block > 26:
            return jnp.zeros((64, 64), WIDE)
        start = (block // 3) * 256 + (192, 0, 64)[block % 3]
        return grad[start:start + 64]

    for block in range(14):
        both = jnp.concatenate([second_block(block), second_block(block + 14)], axis=1)
        grads_b[block * 4:(block + 1) * 4] = both.reshape(4, ROWS, LANES)

    sums = {}
    for dx in range(3):
        for dy in range(3):
            cells = [((1 if dx == 0 else 0) + a, (1 if dy == 0 else 0) + b) for a, b in OWN]
            stacked = jnp.concatenate([d2s[a * 3 + b].astype(LOW) for a, b in cells], axis=0)
            tap = (dx * 3 + dy) * 256
            back = dot(stacked, second[tap:tap + 256], transposed=True)
            for index, (a, b) in enumerate(cells):
                place = (2 * a + dx - 1, 2 * b + dy - 1)
                part = back[index * 32:(index + 1) * 32]
                sums[place] = sums[place] + part if place in sums else part
    for a in range(4):
        for b in range(4):
            total = sums[a, b]
            value = g1[b, a * 32:(a + 1) * 32] * (total[:, 0:128] + up(total[:, 128:256]))
            d1[b * 128 + a * 32:b * 128 + (a + 1) * 32, :] = value.astype(LOW)
    grad = dot(c1t[...], d1[...])
    for dz in range(3):
        start = (0, SLOT, 2 * SLOT)[dz]
        other = (2 * SLOT, 128, 128 + SLOT)[dz]
        w1c[dz * SLOT:(dz + 1) * SLOT, :] = jnp.concatenate(
            [grad[start:start + SLOT, 0:64] + grad[other:other + SLOT, 64:128], jnp.zeros((SLOT, 64), WIDE)], axis=1)
    w1c[120:128, :] = jnp.zeros((8, 128), WIDE)
    grads_b[SECOND_UNITS:SECOND_UNITS + FIRST_UNITS] = w1c[0:128, :].reshape(FIRST_UNITS, ROWS, LANES)

    small.start_swap()
    large.start_depth()
    small.start_plane()
    small.start_depth()
    large.start_final()
    large.start_gather()
    small.start_gather()
    large.pass_on()
    small.pass_on()
    total = large.finish()
    for lanes in range(2):
        out3[:, lanes * 128:(lanes + 1) * 128] = total[lanes * 108:(lanes + 1) * 108].reshape(1728, LANES)
    total = small.finish()
    both = total[0:SECOND_UNITS].reshape(896, LANES)
    out2[0:896, :] = both[:, 0:64]
    out2[896:1728, :] = both[0:832, 64:128]
    w1c[0:128, :] = total[SECOND_UNITS:SECOND_UNITS + FIRST_UNITS].reshape(128, LANES).astype(WIDE)
    for dx in range(3):
        for dy in range(3):
            for dz in range(3):
                out1[dx, dy, dz] = w1c[pl.ds(dz * SLOT + (dx * 3 + dy) * 4, 4), 0:64]
    volumes.sent()
    slopes.sent()
    deltas.sent()


def local(sizes, volume, cotangent, first_weight, second_weight, third_weight):
    dp, size_x, size_y = sizes
    plane = min(4, size_y // CORES) * dp
    depth = size_x * (size_y // (CORES * min(4, size_y // CORES)))
    grain = CORES * plane
    units_a = -(-THIRD_UNITS // grain) * grain
    units_b = -(-(FIRST_UNITS + SECOND_UNITS) // grain) * grain
    kept = cotangent.shape[1]
    spread = size_x * kept * ROWS
    vmem, sems = pltpu.VMEM, pltpu.SemaphoreType.DMA
    mixed = CORES * min(4, size_y // CORES)
    whole, far = pl.BlockSpec(memory_space=pltpu.VMEM), pl.BlockSpec(memory_space=pltpu.HBM)
    grads = pl.pallas_call(
        functools.partial(kernel, sizes),
        out_shape=(
            pltpu.VMEM((3, 3, 3, 4, 64), WIDE),
            pltpu.VMEM((1728, 64), LOW),
            pltpu.VMEM((1728, 256), LOW),
        ),
        in_specs=[far] * 6,
        out_specs=(whole, whole, whole),
        scratch_shapes=[
            vmem((256, 128), LOW), vmem((256, 128), LOW), vmem((256, 128), LOW), vmem((256, 128), LOW),
            vmem(cotangent.shape[1:], LOW), vmem(first_weight.shape, LOW), vmem((256, 128), WIDE), vmem((3, 3, 4, 64, 64), LOW), vmem((3, 3, 4, 64, 256), LOW), vmem((768, 896), LOW),
            sems((8,)), sems((2, 9)),
            vmem((mixed, 8, spread), WIDE), vmem((mixed, 8, spread), WIDE), sems((2, mixed)),
            vmem((depth, mixed, kept * ROWS), WIDE), vmem((depth, mixed, kept * ROWS), WIDE), sems((2, depth)),
            vmem((8, 136, 128), WIDE), vmem((5, 256, 128), LOW), vmem((7, 224, 256), LOW), vmem((4, 128, 128), WIDE),
            vmem((7, 224, 128), LOW), vmem((7, 224, 128), LOW), vmem((288, 2304), LOW), vmem((288, 64), WIDE),
            vmem((4, 16, 128), WIDE), vmem((2, 16, 128), WIDE),
            vmem((2, 16, 128), WIDE), vmem((2, 16, 128), WIDE), vmem((1, 16, 128), WIDE),
            vmem((16, 2304), WIDE), vmem((16, 256), LOW), vmem((16, 256), LOW), vmem((16, 256), LOW), vmem((16, 256), LOW),
            vmem((2304, 128), LOW), vmem((256, 512), LOW), vmem((9, 32, 64), WIDE), vmem((512, 128), LOW),
            vmem((units_a, ROWS, LANES), WIDE), vmem((units_b, ROWS, LANES), WIDE),
            *Reduction.scratch(units_a, plane, depth, False), *Reduction.scratch(units_b, plane, depth, True),
        ],
        compiler_params=pltpu.CompilerParams(collective_id=1, has_side_effects=True, vmem_limit_bytes=60 * 2**20),
        cost_estimate=pl.CostEstimate(flops=1_000_000_000, bytes_accessed=8_000_000, transcendentals=1_000_000),
    )(volume.reshape(256, 128), cotangent[0], first_weight, second_weight, third_weight, jnp.asarray(selection(), LOW))
    return (
        grads[0],
        grads[1].astype(WIDE).reshape(3, 3, 3, 64, 64),
        grads[2].astype(WIDE).reshape(3, 3, 3, 64, 256),
    )


def solution(mesh):
    sizes = tuple(mesh.shape[name] for name in ("dp", "sx", "sy"))
    placed = (P("dp", None, "sx", "sy", None), P("dp", ("sx", "sy"), None, None, None), P(), P(), P())
    return jax.shard_map(
        functools.partial(local, sizes), mesh=mesh, in_specs=placed, out_specs=(P(), P(), P()), check_vma=False)
```

```python
import functools

import jax
import jax.numpy as jnp
import numpy as np
from jax import lax
from jax.experimental import pallas as pl
from jax.experimental.pallas import tpu as pltpu
from jax.sharding import PartitionSpec as P

MESH = pl.DeviceIdType.MESH
LOW, WIDE = jnp.bfloat16, jnp.float32
CORES = 2
ROWS, LANES = 16, 128
SLOT = 40
FIRST_UNITS, SECOND_UNITS, THIRD_UNITS = 8, 56, 216
OWN = ((0, 0), (0, 1), (1, 0), (1, 1))
CELLS = [(1 + a, 1 + b) for a, b in OWN] + [(0, 0), (0, 1), (0, 2), (1, 0), (2, 0)]


def selection():
    result = np.zeros((3, 2, 2, 4, 16, 7, LANES), np.float32)
    for offset in range(3):
        for dx, (pair, odd) in enumerate(((1, 1), (0, 0), (0, 1))):
            for channel in range(4):
                for cell in range(7):
                    for dy in range(3):
                        lane = offset * SLOT + (dx * 3 + dy) * 4 + channel
                        result[offset, pair, odd, channel, 2 * cell + dy + 1, cell, lane] = 1
    return result.reshape(768, 7 * LANES)


def gelu_parts(v):
    square = v * v
    t = jnp.tanh(np.sqrt(2 / np.pi) * (v + 0.044715 * (v * square)))
    return t, square


def gelu(v):
    t, _ = gelu_parts(v)
    return 0.5 * v * (1 + t)


def gelu_slope(v):
    t, square = gelu_parts(v)
    return 0.5 * (1 + t) + 0.5 * v * (1 - t * t) * (np.sqrt(2 / np.pi) * (1 + 3 * 0.044715 * square))


def dot(a, b, transposed=False):
    return lax.dot_general(a, b, (((1,), (1 if transposed else 0,)), ((), ())), preferred_element_type=WIDE)


def down(v, period):
    row = lax.broadcasted_iota(jnp.int32, v.shape, 0)
    return jnp.where((row & (period - 1)) == 0, 0.0, pltpu.roll(v, 1, axis=0))


def up(v):
    row = lax.broadcasted_iota(jnp.int32, v.shape, 0)
    return jnp.where(row == v.shape[0] - 1, 0.0, pltpu.roll(v, v.shape[0] - 1, axis=0))


class Place:
    def __init__(self, dp, sx, sy):
        self.chips_x = min(4, sy // CORES)
        self.low_z, self.chips_y = sx, dp
        self.shift_y, self.shift_z = dp.bit_length() - 1, sx.bit_length() - 1
        self.plane = self.chips_x * dp
        self.depth = sx * (sy // (CORES * self.chips_x))
        self.y, self.sx, self.sy = (lax.axis_index(name) for name in ("dp", "sx", "sy"))
        self.core = lax.rem(self.sy, CORES)
        self.p = lax.rem(self.sy // CORES, self.chips_x) * dp + self.y
        self.mixed = CORES * self.chips_x
        self.t = lax.rem(self.sy, self.mixed)
        self.z = (self.sy // self.mixed) * sx + self.sx

    def device(self, core=None, p=None, z=None):
        core = self.core if core is None else core
        p = self.p if p is None else p
        z = self.z if z is None else z
        chip_x, y = p >> self.shift_y, p & (self.chips_y - 1)
        high, low = z >> self.shift_z, z & (self.low_z - 1)
        return (y, low, (high * self.chips_x + chip_x) * CORES + core)


def others(count, me, body):
    for distance in sorted(range(1, count), key=lambda step: -min(step, count - step)):
        body((me + distance) & (count - 1))


def copy(source, target, sems, at, there, device):
    return pltpu.make_async_remote_copy(
        src_ref=source, dst_ref=target, send_sem=sems.at[0, at], recv_sem=sems.at[1, there],
        device_id=device, device_id_type=MESH)


class Reduction:
    def __init__(self, here, grads, refs, direct):
        self.here, self.grads, self.direct = here, grads, direct
        (self.half_out, self.half_in, self.plane_out, self.plane_in, self.depth_out, self.depth_in,
         self.final, self.gathered, self.half_sems, self.plane_sems, self.depth_sems, self.final_sems,
         self.gather_sems, self.pair_sems) = refs
        self.share = self.plane_out.shape[1]
        self.half = here.plane * self.share
        self.partner = here.device(core=1 - here.core)
        owners = [unit * here.depth // self.share for unit in range(self.share)]
        self.owned = [] if direct else [(unit, owner, unit - owners.index(owner)) for unit, owner in enumerate(owners)]

    @staticmethod
    def scratch(units, plane, depth, direct):
        share = units // (CORES * plane)
        slots = share if direct else -(-share // depth)
        unit = (ROWS, LANES)
        return [
            pltpu.VMEM((plane * share, *unit), LOW),
            pltpu.VMEM((plane * share, *unit), LOW),
            pltpu.VMEM((plane, share, *unit), LOW),
            pltpu.VMEM((plane, share, *unit), LOW),
            pltpu.VMEM((share, *unit), LOW),
            pltpu.VMEM((depth, slots, *unit) if direct else (slots, depth, *unit), LOW),
            pltpu.VMEM((share, *unit), LOW),
            pltpu.VMEM((CORES, plane, share, *unit), LOW),
            pltpu.SemaphoreType.DMA((2, 1)),
            pltpu.SemaphoreType.DMA((2, plane)),
            pltpu.SemaphoreType.DMA((2, max(share, slots * depth))),
            pltpu.SemaphoreType.DMA((2, max(share, slots * depth))),
            pltpu.SemaphoreType.DMA((2, plane)),
            pltpu.SemaphoreType.DMA((2, plane)),
        ]

    def swap(self):
        return copy(self.half_out, self.half_in, self.half_sems, 0, 0, self.partner)

    def start_swap(self):
        self.half_out[...] = self.grads[pl.ds((1 - self.here.core) * self.half, self.half)].astype(LOW)
        self.swap().start()

    def to_plane(self, q, source_slot):
        here = self.here
        return copy(self.plane_out.at[q], self.plane_in.at[source_slot], self.plane_sems, q, source_slot, here.device(p=q))

    def start_plane(self):
        here = self.here
        self.swap().wait()
        mine = self.grads[pl.ds(here.core * self.half, self.half)]
        self.plane_out[...] = (mine + self.half_in[...].astype(WIDE)).astype(LOW).reshape(self.plane_out.shape)
        others(here.plane, here.p, lambda q: self.to_plane(q, here.p).start())

    def to_depth(self, unit, owner, slot, q):
        here = self.here
        return copy(self.depth_out.at[unit], self.depth_in.at[slot, q], self.depth_sems, unit,
                    slot * here.depth + q, here.device(z=owner))

    def start_depth(self):
        here = self.here
        self.plane_in[here.p] = self.plane_out[here.p]
        others(here.plane, here.p, lambda q: self.to_plane(q, q).wait())
        self.depth_out[...] = jnp.sum(self.plane_in[...].astype(WIDE), axis=0).astype(LOW)
        if self.direct:
            others(here.depth, here.z, lambda q: self.to_all(q, here.z).start())
            return
        for unit, owner, slot in self.owned:
            @pl.when(here.z != owner)
            def _():
                self.to_depth(unit, owner, slot, here.z).start()

    def to_all(self, q, source_slot):
        here = self.here
        return copy(self.depth_out, self.depth_in.at[source_slot], self.depth_sems, q, source_slot, here.device(z=q))

    def to_final(self, unit, slot, q):
        here = self.here
        return copy(self.final.at[unit], self.final.at[unit], self.final_sems, slot * here.depth + q, unit, here.device(z=q))

    def start_final(self):
        here = self.here
        for unit, owner, slot in self.owned:
            @pl.when(here.z == owner)
            def _():
                self.depth_in[slot, owner] = self.depth_out[unit]
                others(here.depth, here.z, lambda q: self.to_depth(unit, q, slot, q).wait_recv())
                self.final[unit] = jnp.sum(self.depth_in[slot].astype(WIDE), axis=0).astype(LOW)
                others(here.depth, here.z, lambda q: self.to_final(unit, slot, q).start())

    def to_gather(self, q, source_slot):
        here = self.here
        return copy(self.final, self.gathered.at[here.core, source_slot], self.gather_sems, q, source_slot, here.device(p=q))

    def to_pair(self, core, q):
        return copy(self.gathered.at[core, q], self.gathered.at[core, q], self.pair_sems, q, q, self.partner)

    def start_gather(self):
        here = self.here
        if self.direct:
            self.depth_in[here.z] = self.depth_out[...]
            others(here.depth, here.z, lambda q: self.to_all(q, q).wait())
            self.final[...] = jnp.sum(self.depth_in[...].astype(WIDE), axis=0).astype(LOW)
        for unit, owner, slot in self.owned:
            @pl.when(here.z != owner)
            def _():
                self.to_depth(unit, owner, slot, here.z).wait_send()
                self.to_final(unit, slot, owner).wait_recv()

        others(here.plane, here.p, lambda q: self.to_gather(q, here.p).start())
        self.gathered[here.core, here.p] = self.final[...]
        self.to_pair(here.core, here.p).start()

    def pass_on(self):
        here = self.here

        def step(q):
            self.to_gather(q, q).wait_recv()
            self.to_pair(here.core, q).start()

        others(here.plane, here.p, step)

    def finish(self):
        here = self.here
        for unit, owner, slot in self.owned:
            @pl.when(here.z == owner)
            def _():
                others(here.depth, here.z, lambda q: self.to_final(unit, slot, q).wait_send())

        others(here.plane, here.p, lambda q: self.to_gather(q, q).wait_send())

        for q in range(here.plane):
            self.to_pair(1 - here.core, q).wait()
        return self.gathered[...].reshape(-1, ROWS, LANES)


class Halo:
    def __init__(self, here, sizes, step, sems, first, triples, needs=None):
        self.items = []
        for index, (along_x, along_y, source, target) in enumerate(triples):
            sends = receives = needs
            for along, place, size in ((along_x, here.sx, sizes[1]), (along_y, here.sy, sizes[2])):
                if not along:
                    continue
                ahead, behind = place < size - 1, place > 0
                send, receive = (ahead, behind) if step > 0 else (behind, ahead)
                sends = send if sends is None else jnp.logical_and(sends, send)
                receives = receive if receives is None else jnp.logical_and(receives, receive)
            device = (here.y, here.sx + step * along_x, here.sy + step * along_y)
            move = copy(source, target, sems, first + index, first + index, device)
            self.items.append((sends, receives, move, target))

    def start(self, first=0, last=None):
        for sends, _, move, _ in self.items[first:last]:
            @pl.when(sends)
            def _():
                move.start()

    def wait(self, first=0, last=None):
        for _, receives, move, target in self.items[first:last]:
            @pl.when(receives)
            def _():
                move.wait_recv()

            @pl.when(jnp.logical_not(receives))
            def _():
                target[...] = jnp.zeros(target.shape, target.dtype)

    def sent(self):
        for sends, _, move, _ in self.items:
            @pl.when(sends)
            def _():
                move.wait_send()


def kernel(sizes, volume_hbm, cotangent_hbm, w1_hbm, w2, w3, select, sum_a, sum_b,
           volume, vx, vy, vc, cotangent, w1, w1c, w2s, w3s, sel, local_sems, halo_sems, s1, r1, r1_sems, s2, r2, r2_sems,
           dts, xoff, c1, g1, act1, act1s, lhs2, pre2, g2, g2x, g2y, g2x_in, g2y_in, g2c_in, lhs3, d3, d3x, d3y, d3c,
           lhs2t, c1t, d2s, d1, grads_a, grads_b, *reductions):
    here = Place(*sizes)
    _, size_x, size_y = sizes
    mixed, depth = here.mixed, here.depth
    kept, high = cotangent.shape[0], size_y // mixed

    barrier = pltpu.get_barrier_semaphore()

    def greet(device):
        pl.semaphore_signal(barrier, inc=1, device_id=device, device_id_type=MESH)

    def at_mixed(t):
        return (here.y, here.sx, here.sy - here.t + t)

    expected = depth + mixed + here.plane - 3
    for along_x in range(2):
        for step in (-1, 1):
            inside = here.sy > 0 if step < 0 else here.sy < size_y - 1
            if along_x:
                inside = jnp.logical_and(inside, here.sx > 0 if step < 0 else here.sx < size_x - 1)
            expected = expected + inside.astype(jnp.int32)

            @pl.when(inside)
            def _():
                greet((here.y, here.sx + step * along_x, here.sy + step))

    others(depth, here.z, lambda q: greet(here.device(z=q)))
    others(mixed, here.t, lambda q: greet(at_mixed(q)))
    others(here.plane, here.p, lambda q: greet(here.device(p=q)))
    loads = [
        pltpu.make_async_copy(w1_hbm, w1, local_sems.at[0]),
        pltpu.make_async_copy(cotangent_hbm, cotangent, local_sems.at[1]),
        pltpu.make_async_copy(volume_hbm, volume, local_sems.at[2]),
        pltpu.make_async_copy(select, sel, local_sems.at[3]),
        pltpu.make_async_copy(w2.at[:, :, pl.ds(1, 2)], w2s.at[:, :, pl.ds(0, 2)], local_sems.at[4]),
        pltpu.make_async_copy(w2.at[:, :, pl.ds(0, 1)], w2s.at[:, :, pl.ds(3, 1)], local_sems.at[5]),
        pltpu.make_async_copy(w3.at[:, :, pl.ds(1, 2)], w3s.at[:, :, pl.ds(0, 2)], local_sems.at[6]),
        pltpu.make_async_copy(w3.at[:, :, pl.ds(0, 1)], w3s.at[:, :, pl.ds(3, 1)], local_sems.at[7]),
    ]
    for load in loads:
        load.start()
    for ref in (w2s, w3s):
        ref[:, :, 2] = jnp.zeros((3, 3, *ref.shape[3:]), LOW)
    for index in range(8):
        dts[index, 0:8, :] = jnp.zeros((8, 128), WIDE)
    w1c[...] = jnp.zeros(w1c.shape, WIDE)
    blank = jnp.zeros((4, 64), WIDE)

    loads[0].wait()
    for offset in range(5):
        base = offset * SLOT if offset < 3 else 128 + (offset - 3) * SLOT
        for dx in range(3):
            for dy in range(3):
                left = w1[dx, dy, offset].astype(WIDE) if offset <= 2 else blank
                right = w1[dx, dy, offset - 2].astype(WIDE) if offset >= 2 else blank
                w1c[pl.ds(base + (dx * 3 + dy) * 4, 4), :] = jnp.concatenate([left, right], axis=1)

    loads[1].wait()
    spread = size_x * kept * ROWS
    lane = lax.broadcasted_iota(jnp.int32, (ROWS, spread), 1)
    row = lax.broadcasted_iota(jnp.int32, (ROWS, spread), 0)
    repeat = jnp.where((lane & (ROWS - 1)) == row, 1.0, 0.0).astype(LOW)
    wide = dot(cotangent[...].reshape(kept * size_x * size_y, ROWS), repeat).reshape(kept * size_x, size_y, spread)
    lane = lax.broadcasted_iota(jnp.int32, wide.shape, 2)
    group = lax.broadcasted_iota(jnp.int32, wide.shape, 0)
    strips = jnp.sum(jnp.where((lane >> 4) == lax.rem(group, size_x) * kept + group // size_x, wide, 0.0), axis=0)
    rows = 8 // high
    for t in range(mixed):
        for part in range(high):
            y = part * mixed + t
            s1[t, part * rows:(part + 1) * rows, :] = jnp.broadcast_to(strips[y:y + 1, :], (rows, spread))

    pl.semaphore_wait(barrier, expected)
    pieces = [pl.ds(64 * channel, 64) for channel in range(4)]
    volumes = Halo(here, sizes, 1, halo_sems, 0, (
        *((0, 1, volume_hbm.at[piece], vy.at[piece]) for piece in pieces), (1, 0, volume_hbm, vx)))
    corners = Halo(here, sizes, 1, halo_sems, 5, [(1, 0, vy.at[piece], vc.at[piece]) for piece in pieces], here.sy > 0)
    volumes.start()

    def to_mixed(q, source_slot):
        return copy(s1.at[q], r1.at[source_slot], r1_sems, q, source_slot, at_mixed(q))

    def to_cell(q, source_slot):
        return copy(s2.at[q], r2.at[source_slot], r2_sems, q, source_slot, here.device(z=q))

    others(mixed, here.t, lambda q: to_mixed(q, here.t).start())
    r1[here.t] = s1[here.t]
    others(mixed, here.t, lambda q: to_mixed(q, q).wait())
    for part in range(high):
        strips = jnp.max(r1[:, part * rows:(part + 1) * rows, :], axis=1)
        for x in range(size_x):
            s2[part * size_x + x] = strips[:, x * kept * ROWS:(x + 1) * kept * ROWS]
    others(depth, here.z, lambda q: to_cell(q, here.z).start())
    r2[here.z] = s2[here.z]

    for part in range(4):
        volumes.wait(part, part + 1)
        corners.start(part, part + 1)
    for load in loads[2:4]:
        load.wait()
    volumes.wait(4)
    corners.wait()

    for pair in range(8):
        before, inside = (vc, vx) if pair < 4 else (vy, volume)
        tiles = []
        for channel in range(4):
            at = channel * 64 + (pair % 4) * 16
            tiles.append([ref[at:at + 16, :].astype(WIDE) for ref in (before, inside)])
        ordered = [both[odd * 8:(odd + 1) * 8] for odd in range(2) for refs in tiles for both in refs]
        dts[pair, 8:136, :] = jnp.concatenate(ordered, axis=0).T
    for offset in range(5):
        for pair in range(8):
            xoff[offset, pair * 32:(pair + 1) * 32, :] = dts[pair, pl.ds(7 + offset, 32, stride=4), :].astype(LOW)
    for part, offsets in enumerate(((0, 1, 2), (3, 4))):
        blocks = []
        for offset in offsets:
            blocks += [xoff[offset, 32:256, :], xoff[offset, 0:224, :]]
        chosen = dot(jnp.concatenate(blocks, axis=1), sel[0:256 * len(offsets), :])
        for cell in range(7):
            c1[cell, :, part * 128:(part + 1) * 128] = chosen[:, cell * 128:(cell + 1) * 128].astype(LOW)
    first = w1c[...].astype(LOW)
    for cell in range(7):
        pre = dot(c1[cell], first)
        if cell >= 3:
            g1[cell - 3] = gelu_slope(pre[96:224])
        act = gelu(pre)
        act1[cell] = act.astype(LOW)
        act1s[cell] = down(act, 32).astype(LOW)

    for index, (x, y) in enumerate(CELLS):
        for dx in range(3):
            for dy in range(3):
                at = (dx * 3 + dy) * 256
                rows = slice((2 * x + dx) * 32, (2 * x + dx + 1) * 32)
                lhs2[index * 32:(index + 1) * 32, at:at + 128] = act1[2 * y + dy, rows, :]
                lhs2[index * 32:(index + 1) * 32, at + 128:at + 256] = act1s[2 * y + dy, rows, :]
    for load in loads[4:6]:
        load.wait()
    second = w2s[...].reshape(2304, 64)
    pre2[...] = dot(lhs2[...], second)
    for index, (x, y) in enumerate(CELLS):
        pre = jnp.concatenate(
            [pre2[pl.ds(index * 32 + parity, 16, stride=2), :] for parity in range(2)], axis=1)
        if index < 4:
            slope = gelu_slope(pre)
            g2[index] = slope
            if index < 2:
                g2x[index] = slope.astype(LOW)
            if index in (0, 2):
                g2y[index // 2] = slope.astype(LOW)
        act = gelu(pre)
        at = (x * 3 + y) * 256
        lhs3[:, at:at + 128] = act
        lhs3[:, at + 128:at + 256] = down(act, 16)
    slopes = Halo(here, sizes, -1, halo_sems, 9, (
        (0, 1, g2y, g2y_in), (1, 1, g2x.at[pl.ds(0, 1)], g2c_in), (1, 0, g2x, g2x_in)))
    slopes.start()

    others(depth, here.z, lambda q: to_cell(q, q).wait())
    strips = r2[...].reshape(depth * mixed, kept * ROWS).T.astype(LOW)
    sender = lax.broadcasted_iota(jnp.int32, (depth * mixed, 256), 0)
    channel = lax.broadcasted_iota(jnp.int32, (depth * mixed, 256), 1)
    z, t = sender // mixed, lax.rem(sender, mixed)
    channel = channel - ((lax.rem(z, size_x) * size_y + (z // size_x) * mixed + t) * kept)
    upstream = 0.0
    for k in range(kept):
        choose = jnp.where(channel == k, 1.0, 0.0).astype(LOW)
        upstream = upstream + dot(strips[k * ROWS:(k + 1) * ROWS], choose)
    for load in loads[6:8]:
        load.wait()
    third = w3s[...].reshape(2304, 256)
    pre = dot(lhs3[...].astype(LOW), third)
    delta = (gelu_slope(pre) * upstream).astype(LOW)
    d3[...] = delta
    deltas = Halo(here, sizes, -1, halo_sems, 12, ((0, 1, d3, d3y), (1, 1, d3, d3c), (1, 0, d3, d3x)))
    deltas.start()

    for tap in range(9):
        turned = lhs3[:, tap * 256:(tap + 1) * 256].T.astype(LOW)
        grad = dot(turned, delta)
        for dz, rows in enumerate((192, 0, 64)):
            for lanes in range(2):
                at = lanes * 108 + (tap * 3 + dz) * 4
                grads_a[at:at + 4] = grad[rows:rows + 64, lanes * 128:(lanes + 1) * 128].reshape(4, ROWS, LANES)
    spare = grads_a.shape[0] - THIRD_UNITS
    if spare:
        grads_a[THIRD_UNITS:] = jnp.zeros((spare, ROWS, LANES), WIDE)
    many = len(reductions) // 2
    large = Reduction(here, grads_a, reductions[:many], False)
    small = Reduction(here, grads_b, reductions[many:], True)
    large.start_swap()

    for block in range(18):
        lhs2t[block * 128:(block + 1) * 128, :] = lhs2[0:128, block * 128:(block + 1) * 128].astype(WIDE).T.astype(LOW)
    for cell in range(4):
        for half in range(2):
            lanes = slice(half * 128, (half + 1) * 128)
            c1t[lanes, cell * 128:(cell + 1) * 128] = c1[3 + cell, 96:224, lanes].astype(WIDE).T.astype(LOW)

    large.start_plane()
    slopes.wait()
    deltas.wait()

    sources = {(0, 0): 0, (1, 0): 1, (0, 1): 2, (1, 1): 3}
    back = dot(jnp.concatenate([d3[...], d3x[...], d3y[...], d3c[...]], axis=0), third, transposed=True)
    reads = {0: ((0, 1),), 1: ((0, 2), (1, 0)), 2: ((1, 1),)}
    slope_at = {(0, 0): g2.at[0], (0, 1): g2.at[1], (1, 0): g2.at[2], (1, 1): g2.at[3],
                (2, 0): g2x_in.at[0], (2, 1): g2x_in.at[1], (0, 2): g2y_in.at[0], (1, 2): g2y_in.at[1],
                (2, 2): g2c_in.at[0]}
    for a in range(3):
        for b in range(3):
            total = 0.0
            for from_x, dx in reads[a]:
                for from_y, dy in reads[b]:
                    at, tap = sources[from_x, from_y] * 16, (dx * 3 + dy) * 256
                    total = total + back[at:at + 16, tap:tap + 256]
            value = slope_at[a, b][...].astype(WIDE) * (total[:, 0:128] + up(total[:, 128:256]))
            d2s[a * 3 + b, pl.ds(0, 16, stride=2), :] = value[:, 0:64]
            d2s[a * 3 + b, pl.ds(1, 16, stride=2), :] = value[:, 64:128]

    delta = jnp.concatenate([d2s[a * 3 + b].astype(LOW) for a, b in OWN], axis=0)
    grad = dot(lhs2t[...], delta)

    def second_block(block):
        if block > 26:
            return jnp.zeros((64, 64), WIDE)
        start = (block // 3) * 256 + (192, 0, 64)[block % 3]
        return grad[start:start + 64]

    for block in range(14):
        both = jnp.concatenate([second_block(block), second_block(block + 14)], axis=1)
        grads_b[block * 4:(block + 1) * 4] = both.reshape(4, ROWS, LANES)

    sums = {}
    for dx in range(3):
        for dy in range(3):
            cells = [((1 if dx == 0 else 0) + a, (1 if dy == 0 else 0) + b) for a, b in OWN]
            stacked = jnp.concatenate([d2s[a * 3 + b].astype(LOW) for a, b in cells], axis=0)
            tap = (dx * 3 + dy) * 256
            back = dot(stacked, second[tap:tap + 256], transposed=True)
            for index, (a, b) in enumerate(cells):
                place = (2 * a + dx - 1, 2 * b + dy - 1)
                part = back[index * 32:(index + 1) * 32]
                sums[place] = sums[place] + part if place in sums else part
    for a in range(4):
        for b in range(4):
            total = sums[a, b]
            value = g1[b, a * 32:(a + 1) * 32] * (total[:, 0:128] + up(total[:, 128:256]))
            d1[b * 128 + a * 32:b * 128 + (a + 1) * 32, :] = value.astype(LOW)
    grad = dot(c1t[...], d1[...])
    for dz in range(3):
        start = (0, SLOT, 2 * SLOT)[dz]
        other = (2 * SLOT, 128, 128 + SLOT)[dz]
        w1c[dz * SLOT:(dz + 1) * SLOT, :] = jnp.concatenate(
            [grad[start:start + SLOT, 0:64] + grad[other:other + SLOT, 64:128], jnp.zeros((SLOT, 64), WIDE)], axis=1)
    w1c[120:128, :] = jnp.zeros((8, 128), WIDE)
    grads_b[SECOND_UNITS:SECOND_UNITS + FIRST_UNITS] = w1c[0:128, :].reshape(FIRST_UNITS, ROWS, LANES)

    small.start_swap()
    large.start_depth()
    small.start_plane()
    large.start_final()
    small.start_depth()
    large.start_gather()
    small.start_gather()
    large.pass_on()
    small.pass_on()
    sum_a[...] = large.finish()
    sum_b[...] = small.finish()
    volumes.sent()
    corners.sent()
    slopes.sent()
    deltas.sent()


def unpack_kernel(sum_a, sum_b, out1, out2, out3, first, second, third, sems):
    for lanes in range(2):
        third[:, lanes * 128:(lanes + 1) * 128] = sum_a[lanes * 108:(lanes + 1) * 108].reshape(1728, LANES).astype(WIDE)
    copies = [pltpu.make_async_copy(third, out3, sems.at[0])]
    copies[0].start()
    both = sum_b[0:SECOND_UNITS].reshape(896, LANES).astype(WIDE)
    second[0:896, :] = both[:, 0:64]
    second[896:1728, :] = both[0:832, 64:128]
    copies.append(pltpu.make_async_copy(second, out2, sems.at[1]))
    copies[1].start()
    rows = sum_b[SECOND_UNITS:SECOND_UNITS + FIRST_UNITS].reshape(128, LANES).astype(WIDE)
    for dx in range(3):
        for dy in range(3):
            for dz in range(3):
                at = dz * SLOT + (dx * 3 + dy) * 4
                first[dx, dy, dz] = rows[at:at + 4, 0:64]
    copies.append(pltpu.make_async_copy(first, out1, sems.at[2]))
    copies[2].start()
    for move in copies:
        move.wait()


def unpacked(sums):
    whole, far = pl.BlockSpec(memory_space=pltpu.VMEM), pl.BlockSpec(memory_space=pltpu.HBM)
    shapes = ((3, 3, 3, 4, 64), (1728, 64), (1728, 256))
    return pl.pallas_call(
        unpack_kernel,
        out_shape=tuple(jax.ShapeDtypeStruct(shape, WIDE) for shape in shapes),
        in_specs=[whole] * 2,
        out_specs=(far,) * 3,
        scratch_shapes=[*(pltpu.VMEM(shape, WIDE) for shape in shapes), pltpu.SemaphoreType.DMA((3,))],
        compiler_params=pltpu.CompilerParams(vmem_limit_bytes=16 * 2**20),
    )(*sums)


def local(sizes, volume, cotangent, first_weight, second_weight, third_weight):
    dp, size_x, size_y = sizes
    plane = min(4, size_y // CORES) * dp
    depth = size_x * (size_y // (CORES * min(4, size_y // CORES)))
    grain = CORES * plane
    units_a = -(-THIRD_UNITS // grain) * grain
    units_b = -(-(FIRST_UNITS + SECOND_UNITS) // grain) * grain
    kept = cotangent.shape[1]
    spread = size_x * kept * ROWS
    vmem, sems = pltpu.VMEM, pltpu.SemaphoreType.DMA
    mixed = CORES * min(4, size_y // CORES)
    whole, far = pl.BlockSpec(memory_space=pltpu.VMEM), pl.BlockSpec(memory_space=pltpu.HBM)
    sums = pl.pallas_call(
        functools.partial(kernel, sizes),
        out_shape=(pltpu.VMEM((units_a, ROWS, LANES), LOW), pltpu.VMEM((units_b, ROWS, LANES), LOW)),
        in_specs=[far] * 6,
        out_specs=(whole, whole),
        scratch_shapes=[
            vmem((256, 128), LOW), vmem((256, 128), LOW), vmem((256, 128), LOW), vmem((256, 128), LOW),
            vmem(cotangent.shape[1:], LOW), vmem(first_weight.shape, LOW), vmem((256, 128), WIDE), vmem((3, 3, 4, 64, 64), LOW), vmem((3, 3, 4, 64, 256), LOW), vmem((768, 896), LOW),
            sems((8,)), sems((2, 15)),
            vmem((mixed, 8, spread), WIDE), vmem((mixed, 8, spread), WIDE), sems((2, mixed)),
            vmem((depth, mixed, kept * ROWS), WIDE), vmem((depth, mixed, kept * ROWS), WIDE), sems((2, depth)),
            vmem((8, 136, 128), WIDE), vmem((5, 256, 128), LOW), vmem((7, 224, 256), LOW), vmem((4, 128, 128), WIDE),
            vmem((7, 224, 128), LOW), vmem((7, 224, 128), LOW), vmem((288, 2304), LOW), vmem((288, 64), WIDE),
            vmem((4, 16, 128), WIDE), vmem((2, 16, 128), LOW), vmem((2, 16, 128), LOW),
            vmem((2, 16, 128), LOW), vmem((2, 16, 128), LOW), vmem((1, 16, 128), LOW),
            vmem((16, 2304), WIDE), vmem((16, 256), LOW), vmem((16, 256), LOW), vmem((16, 256), LOW), vmem((16, 256), LOW),
            vmem((2304, 128), LOW), vmem((256, 512), LOW), vmem((9, 32, 64), WIDE), vmem((512, 128), LOW),
            vmem((units_a, ROWS, LANES), WIDE), vmem((units_b, ROWS, LANES), WIDE),
            *Reduction.scratch(units_a, plane, depth, False), *Reduction.scratch(units_b, plane, depth, True),
        ],
        compiler_params=pltpu.CompilerParams(collective_id=1, has_side_effects=True, vmem_limit_bytes=60 * 2**20),
        cost_estimate=pl.CostEstimate(flops=1_000_000_000, bytes_accessed=8_000_000, transcendentals=1_000_000),
    )(volume.reshape(256, 128), cotangent[0], first_weight, second_weight, third_weight, jnp.asarray(selection(), LOW))
    first, second, third = unpacked(sums)
    return first, second.reshape(3, 3, 3, 64, 64), third.reshape(3, 3, 3, 64, 256)


def solution(mesh):
    sizes = tuple(mesh.shape[name] for name in ("dp", "sx", "sy"))
    placed = (P("dp", None, "sx", "sy", None), P("dp", ("sx", "sy"), None, None, None), P(), P(), P())
    return jax.shard_map(
        functools.partial(local, sizes), mesh=mesh, in_specs=placed, out_specs=(P(), P(), P()), check_vma=False)
```

```python
import functools

import jax
import jax.numpy as jnp
import numpy as np
from jax import lax
from jax.experimental import pallas as pl
from jax.experimental.pallas import tpu as pltpu
from jax.sharding import PartitionSpec as P

MESH = pl.DeviceIdType.MESH
LOW, WIDE = jnp.bfloat16, jnp.float32
CORES = 2
ROWS, LANES = 16, 128
SLOT = 40
FIRST_UNITS, SECOND_UNITS, THIRD_UNITS = 8, 56, 216
OWN = ((0, 0), (0, 1), (1, 0), (1, 1))
CELLS = [(1 + a, 1 + b) for a, b in OWN] + [(0, 0), (0, 1), (0, 2), (1, 0), (2, 0)]


def selection():
    result = np.zeros((3, 2, 2, 4, 16, 7, LANES), np.float32)
    for offset in range(3):
        for dx, (pair, odd) in enumerate(((1, 1), (0, 0), (0, 1))):
            for channel in range(4):
                for cell in range(7):
                    for dy in range(3):
                        lane = offset * SLOT + (dx * 3 + dy) * 4 + channel
                        result[offset, pair, odd, channel, 2 * cell + dy + 1, cell, lane] = 1
    return result.reshape(768, 7 * LANES)


def gelu_parts(v):
    square = v * v
    t = jnp.tanh(np.sqrt(2 / np.pi) * (v + 0.044715 * (v * square)))
    return t, square


def gelu(v):
    t, _ = gelu_parts(v)
    return 0.5 * v * (1 + t)


def gelu_slope(v):
    t, square = gelu_parts(v)
    return 0.5 * (1 + t) + 0.5 * v * (1 - t * t) * (np.sqrt(2 / np.pi) * (1 + 3 * 0.044715 * square))


def dot(a, b, transposed=False):
    return lax.dot_general(a, b, (((1,), (1 if transposed else 0,)), ((), ())), preferred_element_type=WIDE)


def down(v, period):
    row = lax.broadcasted_iota(jnp.int32, v.shape, 0)
    return jnp.where((row & (period - 1)) == 0, 0.0, pltpu.roll(v, 1, axis=0))


def up(v):
    row = lax.broadcasted_iota(jnp.int32, v.shape, 0)
    return jnp.where(row == v.shape[0] - 1, 0.0, pltpu.roll(v, v.shape[0] - 1, axis=0))


class Place:
    def __init__(self, dp, sx, sy):
        self.chips_x = min(4, sy // CORES)
        self.low_z, self.chips_y = sx, dp
        self.shift_y, self.shift_z = dp.bit_length() - 1, sx.bit_length() - 1
        self.plane = self.chips_x * dp
        self.depth = sx * (sy // (CORES * self.chips_x))
        self.y, self.sx, self.sy = (lax.axis_index(name) for name in ("dp", "sx", "sy"))
        self.core = lax.rem(self.sy, CORES)
        self.p = lax.rem(self.sy // CORES, self.chips_x) * dp + self.y
        self.mixed = CORES * self.chips_x
        self.t = lax.rem(self.sy, self.mixed)
        self.z = (self.sy // self.mixed) * sx + self.sx

    def device(self, core=None, p=None, z=None):
        core = self.core if core is None else core
        p = self.p if p is None else p
        z = self.z if z is None else z
        chip_x, y = p >> self.shift_y, p & (self.chips_y - 1)
        high, low = z >> self.shift_z, z & (self.low_z - 1)
        return (y, low, (high * self.chips_x + chip_x) * CORES + core)


def others(count, me, body):
    for distance in sorted(range(1, count), key=lambda step: -min(step, count - step)):
        body((me + distance) & (count - 1))


def copy(source, target, sems, at, there, device):
    return pltpu.make_async_remote_copy(
        src_ref=source, dst_ref=target, send_sem=sems.at[0, at], recv_sem=sems.at[1, there],
        device_id=device, device_id_type=MESH)


class Reduction:
    def __init__(self, here, grads, refs, direct):
        self.here, self.grads, self.direct = here, grads, direct
        (self.half_out, self.half_in, self.plane_out, self.plane_in, self.depth_out, self.depth_in,
         self.final, self.gathered, self.half_sems, self.plane_sems, self.depth_sems, self.final_sems,
         self.gather_sems, self.pair_sems) = refs
        self.share = self.plane_out.shape[1]
        self.half = here.plane * self.share
        self.partner = here.device(core=1 - here.core)
        owners = [unit * here.depth // self.share for unit in range(self.share)]
        self.owned = [] if direct else [(unit, owner, unit - owners.index(owner)) for unit, owner in enumerate(owners)]

    @staticmethod
    def scratch(units, plane, depth, direct):
        share = units // (CORES * plane)
        slots = share if direct else -(-share // depth)
        unit = (ROWS, LANES)
        return [
            pltpu.VMEM((plane * share, *unit), LOW),
            pltpu.VMEM((plane * share, *unit), LOW),
            pltpu.VMEM((plane, share, *unit), LOW),
            pltpu.VMEM((plane, share, *unit), LOW),
            pltpu.VMEM((share, *unit), LOW),
            pltpu.VMEM((depth, slots, *unit) if direct else (slots, depth, *unit), LOW),
            pltpu.VMEM((share, *unit), LOW),
            pltpu.VMEM((CORES, plane, share, *unit), LOW),
            pltpu.SemaphoreType.DMA((2, 1)),
            pltpu.SemaphoreType.DMA((2, plane)),
            pltpu.SemaphoreType.DMA((2, max(share, slots * depth))),
            pltpu.SemaphoreType.DMA((2, max(share, slots * depth))),
            pltpu.SemaphoreType.DMA((2, plane)),
            pltpu.SemaphoreType.DMA((2, plane)),
        ]

    def swap(self):
        return copy(self.half_out, self.half_in, self.half_sems, 0, 0, self.partner)

    def start_swap(self):
        self.half_out[...] = self.grads[pl.ds((1 - self.here.core) * self.half, self.half)].astype(LOW)
        self.swap().start()

    def to_plane(self, q, source_slot):
        here = self.here
        return copy(self.plane_out.at[q], self.plane_in.at[source_slot], self.plane_sems, q, source_slot, here.device(p=q))

    def start_plane(self):
        here = self.here
        self.swap().wait()
        if self.grads.shape[0] == self.half:
            mine = self.grads[...]
        else:
            mine = self.grads[pl.ds(here.core * self.half, self.half)]
        self.plane_out[...] = (mine + self.half_in[...].astype(WIDE)).astype(LOW).reshape(self.plane_out.shape)
        others(here.plane, here.p, lambda q: self.to_plane(q, here.p).start())

    def to_depth(self, unit, owner, slot, q):
        here = self.here
        return copy(self.depth_out.at[unit], self.depth_in.at[slot, q], self.depth_sems, unit,
                    slot * here.depth + q, here.device(z=owner))

    def start_depth(self):
        here = self.here
        self.plane_in[here.p] = self.plane_out[here.p]
        others(here.plane, here.p, lambda q: self.to_plane(q, q).wait())
        self.depth_out[...] = jnp.sum(self.plane_in[...].astype(WIDE), axis=0).astype(LOW)
        if self.direct:
            others(here.depth, here.z, lambda q: self.to_all(q, here.z).start())
            return
        for unit, owner, slot in self.owned:
            @pl.when(here.z != owner)
            def _():
                self.to_depth(unit, owner, slot, here.z).start()

    def to_all(self, q, source_slot):
        here = self.here
        return copy(self.depth_out, self.depth_in.at[source_slot], self.depth_sems, q, source_slot, here.device(z=q))

    def to_final(self, unit, slot, q):
        here = self.here
        return copy(self.final.at[unit], self.final.at[unit], self.final_sems, slot * here.depth + q, unit, here.device(z=q))

    def start_final(self):
        here = self.here
        for unit, owner, slot in self.owned:
            @pl.when(here.z == owner)
            def _():
                self.depth_in[slot, owner] = self.depth_out[unit]
                others(here.depth, here.z, lambda q: self.to_depth(unit, q, slot, q).wait_recv())
                self.final[unit] = jnp.sum(self.depth_in[slot].astype(WIDE), axis=0).astype(LOW)
                others(here.depth, here.z, lambda q: self.to_final(unit, slot, q).start())

    def to_gather(self, q, source_slot):
        here = self.here
        return copy(self.final, self.gathered.at[here.core, source_slot], self.gather_sems, q, source_slot, here.device(p=q))

    def to_pair(self, core, q):
        return copy(self.gathered.at[core, q], self.gathered.at[core, q], self.pair_sems, q, q, self.partner)

    def start_gather(self):
        here = self.here
        if self.direct:
            self.depth_in[here.z] = self.depth_out[...]
            others(here.depth, here.z, lambda q: self.to_all(q, q).wait())
            self.final[...] = jnp.sum(self.depth_in[...].astype(WIDE), axis=0).astype(LOW)
        for unit, owner, slot in self.owned:
            @pl.when(here.z != owner)
            def _():
                self.to_depth(unit, owner, slot, here.z).wait_send()
                self.to_final(unit, slot, owner).wait_recv()

        others(here.plane, here.p, lambda q: self.to_gather(q, here.p).start())
        self.gathered[here.core, here.p] = self.final[...]
        self.to_pair(here.core, here.p).start()

    def pass_on(self):
        here = self.here

        def step(q):
            self.to_gather(q, q).wait_recv()
            self.to_pair(here.core, q).start()

        others(here.plane, here.p, step)

    def finish(self):
        here = self.here
        for unit, owner, slot in self.owned:
            @pl.when(here.z == owner)
            def _():
                others(here.depth, here.z, lambda q: self.to_final(unit, slot, q).wait_send())

        others(here.plane, here.p, lambda q: self.to_gather(q, q).wait_send())

        for q in range(here.plane):
            self.to_pair(1 - here.core, q).wait()
        return self.gathered[...].reshape(-1, ROWS, LANES)


class Halo:
    def __init__(self, here, sizes, step, sems, first, triples, needs=None):
        self.items = []
        for index, (along_x, along_y, source, target) in enumerate(triples):
            sends = receives = needs
            for along, place, size in ((along_x, here.sx, sizes[1]), (along_y, here.sy, sizes[2])):
                if not along:
                    continue
                ahead, behind = place < size - 1, place > 0
                send, receive = (ahead, behind) if step > 0 else (behind, ahead)
                sends = send if sends is None else jnp.logical_and(sends, send)
                receives = receive if receives is None else jnp.logical_and(receives, receive)
            device = (here.y, here.sx + step * along_x, here.sy + step * along_y)
            move = copy(source, target, sems, first + index, first + index, device)
            self.items.append((sends, receives, move, target))

    def start(self, first=0, last=None):
        for sends, _, move, _ in self.items[first:last]:
            @pl.when(sends)
            def _():
                move.start()

    def wait(self, first=0, last=None):
        for _, receives, move, target in self.items[first:last]:
            @pl.when(receives)
            def _():
                move.wait_recv()

            @pl.when(jnp.logical_not(receives))
            def _():
                target[...] = jnp.zeros(target.shape, target.dtype)

    def sent(self):
        for sends, _, move, _ in self.items:
            @pl.when(sends)
            def _():
                move.wait_send()


def kernel(sizes, volume_hbm, cotangent_hbm, w1_hbm, w2, w3, select, sum_a, sum_b,
           volume, vx, vy, vc, cotangent, w1, w1c, w2s, w3s, sel, local_sems, halo_sems, s1, r1, r1_sems, s2, r2, r2_sems,
           dts, xoff, c1, g1, act1, act1s, lhs2, pre2, g2, g2x, g2y, g2x_in, g2y_in, g2c_in, lhs3, d3, d3x, d3y, d3c,
           lhs2t, c1t, d2s, d1, grads_a, grads_b, *reductions):
    here = Place(*sizes)
    _, size_x, size_y = sizes
    mixed, depth = here.mixed, here.depth
    kept, high = cotangent.shape[0], size_y // mixed

    barrier = pltpu.get_barrier_semaphore()

    def greet(device):
        pl.semaphore_signal(barrier, inc=1, device_id=device, device_id_type=MESH)

    def at_mixed(t):
        return (here.y, here.sx, here.sy - here.t + t)

    expected = depth + mixed + here.plane - 3
    for along_x in range(2):
        for step in (-1, 1):
            inside = here.sy > 0 if step < 0 else here.sy < size_y - 1
            if along_x:
                inside = jnp.logical_and(inside, here.sx > 0 if step < 0 else here.sx < size_x - 1)
            expected = expected + inside.astype(jnp.int32)

            @pl.when(inside)
            def _():
                greet((here.y, here.sx + step * along_x, here.sy + step))

    others(depth, here.z, lambda q: greet(here.device(z=q)))
    others(mixed, here.t, lambda q: greet(at_mixed(q)))
    others(here.plane, here.p, lambda q: greet(here.device(p=q)))
    loads = [
        pltpu.make_async_copy(w1_hbm, w1, local_sems.at[0]),
        pltpu.make_async_copy(cotangent_hbm, cotangent, local_sems.at[1]),
        pltpu.make_async_copy(volume_hbm, volume, local_sems.at[2]),
        pltpu.make_async_copy(select, sel, local_sems.at[3]),
        pltpu.make_async_copy(w2.at[:, :, pl.ds(1, 2)], w2s.at[:, :, pl.ds(0, 2)], local_sems.at[4]),
        pltpu.make_async_copy(w2.at[:, :, pl.ds(0, 1)], w2s.at[:, :, pl.ds(3, 1)], local_sems.at[5]),
        pltpu.make_async_copy(w3.at[:, :, pl.ds(1, 2)], w3s.at[:, :, pl.ds(0, 2)], local_sems.at[6]),
        pltpu.make_async_copy(w3.at[:, :, pl.ds(0, 1)], w3s.at[:, :, pl.ds(3, 1)], local_sems.at[7]),
    ]
    for load in loads:
        load.start()
    for ref in (w2s, w3s):
        ref[:, :, 2] = jnp.zeros((3, 3, *ref.shape[3:]), LOW)
    for index in range(8):
        dts[index, 0:8, :] = jnp.zeros((8, 128), WIDE)
    w1c[...] = jnp.zeros(w1c.shape, WIDE)
    blank = jnp.zeros((4, 64), WIDE)

    loads[0].wait()
    for offset in range(5):
        base = offset * SLOT if offset < 3 else 128 + (offset - 3) * SLOT
        for dx in range(3):
            for dy in range(3):
                left = w1[dx, dy, offset].astype(WIDE) if offset <= 2 else blank
                right = w1[dx, dy, offset - 2].astype(WIDE) if offset >= 2 else blank
                w1c[pl.ds(base + (dx * 3 + dy) * 4, 4), :] = jnp.concatenate([left, right], axis=1)

    loads[1].wait()
    spread = size_x * kept * ROWS
    lane = lax.broadcasted_iota(jnp.int32, (ROWS, spread), 1)
    row = lax.broadcasted_iota(jnp.int32, (ROWS, spread), 0)
    repeat = jnp.where((lane & (ROWS - 1)) == row, 1.0, 0.0).astype(LOW)
    wide = dot(cotangent[...].reshape(kept * size_x * size_y, ROWS), repeat).reshape(kept * size_x, size_y, spread)
    lane = lax.broadcasted_iota(jnp.int32, wide.shape, 2)
    group = lax.broadcasted_iota(jnp.int32, wide.shape, 0)
    strips = jnp.sum(jnp.where((lane >> 4) == lax.rem(group, size_x) * kept + group // size_x, wide, 0.0), axis=0)
    rows = 8 // high
    for t in range(mixed):
        for part in range(high):
            y = part * mixed + t
            s1[t, part * rows:(part + 1) * rows, :] = jnp.broadcast_to(strips[y:y + 1, :], (rows, spread))

    loads[2].wait()
    pl.semaphore_wait(barrier, expected)
    pieces = [pl.ds(64 * channel, 64) for channel in range(4)]
    volumes = Halo(here, sizes, 1, halo_sems, 0, (
        *((0, 1, volume.at[piece], vy.at[piece]) for piece in pieces), (1, 0, volume, vx)))
    corners = Halo(here, sizes, 1, halo_sems, 5, [(1, 0, vy.at[piece], vc.at[piece]) for piece in pieces], here.sy > 0)
    volumes.start()

    def to_mixed(q, source_slot):
        return copy(s1.at[q], r1.at[source_slot], r1_sems, q, source_slot, at_mixed(q))

    def to_cell(q, source_slot):
        return copy(s2.at[q], r2.at[source_slot], r2_sems, q, source_slot, here.device(z=q))

    others(mixed, here.t, lambda q: to_mixed(q, here.t).start())
    r1[here.t] = s1[here.t]
    others(mixed, here.t, lambda q: to_mixed(q, q).wait())
    for part in range(high):
        strips = jnp.max(r1[:, part * rows:(part + 1) * rows, :], axis=1)
        for x in range(size_x):
            s2[part * size_x + x] = strips[:, x * kept * ROWS:(x + 1) * kept * ROWS]
    others(depth, here.z, lambda q: to_cell(q, here.z).start())
    r2[here.z] = s2[here.z]

    for part in range(4):
        volumes.wait(part, part + 1)
        corners.start(part, part + 1)
    loads[3].wait()
    volumes.wait(4)
    corners.wait()

    for pair in range(8):
        before, inside = (vc, vx) if pair < 4 else (vy, volume)
        tiles = []
        for channel in range(4):
            at = channel * 64 + (pair % 4) * 16
            tiles.append([ref[at:at + 16, :].astype(WIDE) for ref in (before, inside)])
        ordered = [both[odd * 8:(odd + 1) * 8] for odd in range(2) for refs in tiles for both in refs]
        dts[pair, 8:136, :] = jnp.concatenate(ordered, axis=0).T
    for offset in range(5):
        for pair in range(8):
            xoff[offset, pair * 32:(pair + 1) * 32, :] = dts[pair, pl.ds(7 + offset, 32, stride=4), :].astype(LOW)
    for part, offsets in enumerate(((0, 1, 2), (3, 4))):
        blocks = []
        for offset in offsets:
            blocks += [xoff[offset, 32:256, :], xoff[offset, 0:224, :]]
        chosen = dot(jnp.concatenate(blocks, axis=1), sel[0:256 * len(offsets), :])
        for cell in range(7):
            c1[cell, :, part * 128:(part + 1) * 128] = chosen[:, cell * 128:(cell + 1) * 128].astype(LOW)
    first = w1c[...].astype(LOW)
    for cell in range(7):
        pre = dot(c1[cell], first)
        if cell >= 3:
            g1[cell - 3] = gelu_slope(pre[96:224])
        act = gelu(pre)
        act1[cell] = act.astype(LOW)
        act1s[cell] = down(act, 32).astype(LOW)

    for index, (x, y) in enumerate(CELLS):
        for dx in range(3):
            for dy in range(3):
                at = (dx * 3 + dy) * 256
                rows = slice((2 * x + dx) * 32, (2 * x + dx + 1) * 32)
                lhs2[index * 32:(index + 1) * 32, at:at + 128] = act1[2 * y + dy, rows, :]
                lhs2[index * 32:(index + 1) * 32, at + 128:at + 256] = act1s[2 * y + dy, rows, :]
    for load in loads[4:6]:
        load.wait()
    second = w2s[...].reshape(2304, 64)
    pre2[...] = dot(lhs2[...], second)
    for index, (x, y) in enumerate(CELLS):
        pre = jnp.concatenate(
            [pre2[pl.ds(index * 32 + parity, 16, stride=2), :] for parity in range(2)], axis=1)
        if index < 4:
            slope = gelu_slope(pre)
            g2[index] = slope
            if index < 2:
                g2x[index] = slope.astype(LOW)
            if index in (0, 2):
                g2y[index // 2] = slope.astype(LOW)
        act = gelu(pre)
        at = (x * 3 + y) * 256
        lhs3[:, at:at + 128] = act
        lhs3[:, at + 128:at + 256] = down(act, 16)
    slopes = Halo(here, sizes, -1, halo_sems, 9, (
        (0, 1, g2y, g2y_in), (1, 1, g2x.at[pl.ds(0, 1)], g2c_in), (1, 0, g2x, g2x_in)))
    slopes.start()

    others(depth, here.z, lambda q: to_cell(q, q).wait())
    strips = r2[...].reshape(depth * mixed, kept * ROWS).T.astype(LOW)
    sender = lax.broadcasted_iota(jnp.int32, (depth * mixed, 256), 0)
    channel = lax.broadcasted_iota(jnp.int32, (depth * mixed, 256), 1)
    z, t = sender // mixed, lax.rem(sender, mixed)
    channel = channel - ((lax.rem(z, size_x) * size_y + (z // size_x) * mixed + t) * kept)
    upstream = 0.0
    for k in range(kept):
        choose = jnp.where(channel == k, 1.0, 0.0).astype(LOW)
        upstream = upstream + dot(strips[k * ROWS:(k + 1) * ROWS], choose)
    for load in loads[6:8]:
        load.wait()
    third = w3s[...].reshape(2304, 256)
    pre = dot(lhs3[...].astype(LOW), third)
    delta = (gelu_slope(pre) * upstream).astype(LOW)
    d3[...] = delta
    deltas = Halo(here, sizes, -1, halo_sems, 12, ((0, 1, d3, d3y), (1, 1, d3, d3c), (1, 0, d3, d3x)))
    deltas.start()

    many = len(reductions) // 2
    large = Reduction(here, grads_a, reductions[:many], False)
    small = Reduction(here, grads_b, reductions[many:], True)
    turned = [lhs3[:, tap * 256:(tap + 1) * 256].T.astype(LOW) for tap in range(9)]
    halves = [delta[:, lanes * 128:(lanes + 1) * 128].astype(WIDE) for lanes in range(2)]
    even = here.core == 0

    def third_grad(right, target):
        for tap in range(9):
            grad = dot(turned[tap], right.astype(LOW))
            for dz, rows in enumerate((192, 0, 64)):
                at = (tap * 3 + dz) * 4
                target[at:at + 4] = grad[rows:rows + 64].astype(target.dtype).reshape(4, ROWS, LANES)
        spare = target.shape[0] - THIRD_UNITS // 2
        if spare:
            target[THIRD_UNITS // 2:] = jnp.zeros((spare, ROWS, LANES), target.dtype)

    third_grad(jnp.where(even, halves[1], halves[0]), large.half_out)
    large.swap().start()
    third_grad(jnp.where(even, halves[0], halves[1]), grads_a)

    for block in range(18):
        lhs2t[block * 128:(block + 1) * 128, :] = lhs2[0:128, block * 128:(block + 1) * 128].astype(WIDE).T.astype(LOW)
    for cell in range(4):
        for half in range(2):
            lanes = slice(half * 128, (half + 1) * 128)
            c1t[lanes, cell * 128:(cell + 1) * 128] = c1[3 + cell, 96:224, lanes].astype(WIDE).T.astype(LOW)

    large.start_plane()
    slopes.wait()
    deltas.wait()

    sources = {(0, 0): 0, (1, 0): 1, (0, 1): 2, (1, 1): 3}
    back = dot(jnp.concatenate([d3[...], d3x[...], d3y[...], d3c[...]], axis=0), third, transposed=True)
    reads = {0: ((0, 1),), 1: ((0, 2), (1, 0)), 2: ((1, 1),)}
    slope_at = {(0, 0): g2.at[0], (0, 1): g2.at[1], (1, 0): g2.at[2], (1, 1): g2.at[3],
                (2, 0): g2x_in.at[0], (2, 1): g2x_in.at[1], (0, 2): g2y_in.at[0], (1, 2): g2y_in.at[1],
                (2, 2): g2c_in.at[0]}
    for a in range(3):
        for b in range(3):
            total = 0.0
            for from_x, dx in reads[a]:
                for from_y, dy in reads[b]:
                    at, tap = sources[from_x, from_y] * 16, (dx * 3 + dy) * 256
                    total = total + back[at:at + 16, tap:tap + 256]
            value = slope_at[a, b][...].astype(WIDE) * (total[:, 0:128] + up(total[:, 128:256]))
            d2s[a * 3 + b, pl.ds(0, 16, stride=2), :] = value[:, 0:64]
            d2s[a * 3 + b, pl.ds(1, 16, stride=2), :] = value[:, 64:128]

    delta = jnp.concatenate([d2s[a * 3 + b].astype(LOW) for a, b in OWN], axis=0)
    grad = dot(lhs2t[...], delta)

    def second_block(block):
        if block > 26:
            return jnp.zeros((64, 64), WIDE)
        start = (block // 3) * 256 + (192, 0, 64)[block % 3]
        return grad[start:start + 64]

    for block in range(14):
        both = jnp.concatenate([second_block(block), second_block(block + 14)], axis=1)
        grads_b[block * 4:(block + 1) * 4] = both.reshape(4, ROWS, LANES)

    sums = {}
    for dx in range(3):
        for dy in range(3):
            cells = [((1 if dx == 0 else 0) + a, (1 if dy == 0 else 0) + b) for a, b in OWN]
            stacked = jnp.concatenate([d2s[a * 3 + b].astype(LOW) for a, b in cells], axis=0)
            tap = (dx * 3 + dy) * 256
            back = dot(stacked, second[tap:tap + 256], transposed=True)
            for index, (a, b) in enumerate(cells):
                place = (2 * a + dx - 1, 2 * b + dy - 1)
                part = back[index * 32:(index + 1) * 32]
                sums[place] = sums[place] + part if place in sums else part
    for a in range(4):
        for b in range(4):
            total = sums[a, b]
            value = g1[b, a * 32:(a + 1) * 32] * (total[:, 0:128] + up(total[:, 128:256]))
            d1[b * 128 + a * 32:b * 128 + (a + 1) * 32, :] = value.astype(LOW)
    grad = dot(c1t[...], d1[...])
    for dz in range(3):
        start = (0, SLOT, 2 * SLOT)[dz]
        other = (2 * SLOT, 128, 128 + SLOT)[dz]
        w1c[dz * SLOT:(dz + 1) * SLOT, :] = jnp.concatenate(
            [grad[start:start + SLOT, 0:64] + grad[other:other + SLOT, 64:128], jnp.zeros((SLOT, 64), WIDE)], axis=1)
    w1c[120:128, :] = jnp.zeros((8, 128), WIDE)
    grads_b[SECOND_UNITS:SECOND_UNITS + FIRST_UNITS] = w1c[0:128, :].reshape(FIRST_UNITS, ROWS, LANES)

    small.start_swap()
    large.start_depth()
    small.start_plane()
    large.start_final()
    small.start_depth()
    large.start_gather()
    small.start_gather()
    large.pass_on()
    small.pass_on()
    sum_a[...] = large.finish()
    sum_b[...] = small.finish()
    volumes.sent()
    corners.sent()
    slopes.sent()
    deltas.sent()


def unpack_kernel(sum_a, sum_b, out1, out2, out3, first, second, third, sems):
    half = sum_a.shape[0] // 2
    copies = []
    for part in range(3):
        for lanes in range(2):
            at = lanes * half + part * 36
            block = sum_a[at:at + 36].reshape(576, LANES)
            third[part * 576:(part + 1) * 576, lanes * 128:(lanes + 1) * 128] = block.astype(WIDE)
        rows = pl.ds(part * 576, 576)
        copies.append(pltpu.make_async_copy(third.at[rows], out3.at[rows], sems.at[part]))
        copies[part].start()
    both = sum_b[0:SECOND_UNITS].reshape(896, LANES).astype(WIDE)
    second[0:896, :] = both[:, 0:64]
    second[896:1728, :] = both[0:832, 64:128]
    copies.append(pltpu.make_async_copy(second, out2, sems.at[3]))
    copies[3].start()
    rows = sum_b[SECOND_UNITS:SECOND_UNITS + FIRST_UNITS].reshape(128, LANES).astype(WIDE)
    for dx in range(3):
        for dy in range(3):
            for dz in range(3):
                at = dz * SLOT + (dx * 3 + dy) * 4
                first[dx, dy, dz] = rows[at:at + 4, 0:64]
    copies.append(pltpu.make_async_copy(first, out1, sems.at[4]))
    copies[4].start()
    for move in copies:
        move.wait()


def unpacked(sums):
    whole, far = pl.BlockSpec(memory_space=pltpu.VMEM), pl.BlockSpec(memory_space=pltpu.HBM)
    shapes = ((3, 3, 3, 4, 64), (1728, 64), (1728, 256))
    return pl.pallas_call(
        unpack_kernel,
        out_shape=tuple(jax.ShapeDtypeStruct(shape, WIDE) for shape in shapes),
        in_specs=[whole] * 2,
        out_specs=(far,) * 3,
        scratch_shapes=[*(pltpu.VMEM(shape, WIDE) for shape in shapes), pltpu.SemaphoreType.DMA((5,))],
        compiler_params=pltpu.CompilerParams(vmem_limit_bytes=16 * 2**20),
    )(*sums)


def local(sizes, volume, cotangent, first_weight, second_weight, third_weight):
    dp, size_x, size_y = sizes
    plane = min(4, size_y // CORES) * dp
    depth = size_x * (size_y // (CORES * min(4, size_y // CORES)))
    grain = CORES * plane
    units_a = -(-THIRD_UNITS // grain) * grain
    units_b = -(-(FIRST_UNITS + SECOND_UNITS) // grain) * grain
    kept = cotangent.shape[1]
    spread = size_x * kept * ROWS
    vmem, sems = pltpu.VMEM, pltpu.SemaphoreType.DMA
    mixed = CORES * min(4, size_y // CORES)
    whole, far = pl.BlockSpec(memory_space=pltpu.VMEM), pl.BlockSpec(memory_space=pltpu.HBM)
    sums = pl.pallas_call(
        functools.partial(kernel, sizes),
        out_shape=(pltpu.VMEM((units_a, ROWS, LANES), LOW), pltpu.VMEM((units_b, ROWS, LANES), LOW)),
        in_specs=[far] * 6,
        out_specs=(whole, whole),
        scratch_shapes=[
            vmem((256, 128), LOW), vmem((256, 128), LOW), vmem((256, 128), LOW), vmem((256, 128), LOW),
            vmem(cotangent.shape[1:], LOW), vmem(first_weight.shape, LOW), vmem((256, 128), WIDE), vmem((3, 3, 4, 64, 64), LOW), vmem((3, 3, 4, 64, 256), LOW), vmem((768, 896), LOW),
            sems((8,)), sems((2, 15)),
            vmem((mixed, 8, spread), WIDE), vmem((mixed, 8, spread), WIDE), sems((2, mixed)),
            vmem((depth, mixed, kept * ROWS), WIDE), vmem((depth, mixed, kept * ROWS), WIDE), sems((2, depth)),
            vmem((8, 136, 128), WIDE), vmem((5, 256, 128), LOW), vmem((7, 224, 256), LOW), vmem((4, 128, 128), WIDE),
            vmem((7, 224, 128), LOW), vmem((7, 224, 128), LOW), vmem((288, 2304), LOW), vmem((288, 64), WIDE),
            vmem((4, 16, 128), WIDE), vmem((2, 16, 128), LOW), vmem((2, 16, 128), LOW),
            vmem((2, 16, 128), LOW), vmem((2, 16, 128), LOW), vmem((1, 16, 128), LOW),
            vmem((16, 2304), WIDE), vmem((16, 256), LOW), vmem((16, 256), LOW), vmem((16, 256), LOW), vmem((16, 256), LOW),
            vmem((2304, 128), LOW), vmem((256, 512), LOW), vmem((9, 32, 64), WIDE), vmem((512, 128), LOW),
            vmem((units_a // 2, ROWS, LANES), WIDE), vmem((units_b, ROWS, LANES), WIDE),
            *Reduction.scratch(units_a, plane, depth, False), *Reduction.scratch(units_b, plane, depth, True),
        ],
        compiler_params=pltpu.CompilerParams(collective_id=1, has_side_effects=True, vmem_limit_bytes=60 * 2**20),
        cost_estimate=pl.CostEstimate(flops=1_000_000_000, bytes_accessed=8_000_000, transcendentals=1_000_000),
    )(volume.reshape(256, 128), cotangent[0], first_weight, second_weight, third_weight, jnp.asarray(selection(), LOW))
    first, second, third = unpacked(sums)
    return first, second.reshape(3, 3, 3, 64, 64), third.reshape(3, 3, 3, 64, 256)


def solution(mesh):
    sizes = tuple(mesh.shape[name] for name in ("dp", "sx", "sy"))
    placed = (P("dp", None, "sx", "sy", None), P("dp", ("sx", "sy"), None, None, None), P(), P(), P())
    return jax.shard_map(
        functools.partial(local, sizes), mesh=mesh, in_specs=placed, out_specs=(P(), P(), P()), check_vma=False)
```

```python
import functools

import jax
import jax.numpy as jnp
import numpy as np
from jax import lax
from jax.experimental import pallas as pl
from jax.experimental.pallas import tpu as pltpu
from jax.sharding import PartitionSpec as P

MESH = pl.DeviceIdType.MESH
LOW, WIDE = jnp.bfloat16, jnp.float32
CORES = 2
ROWS, LANES = 16, 128
SLOT = 40
FIRST_UNITS, SECOND_UNITS, THIRD_UNITS = 8, 56, 216
OWN = ((0, 0), (0, 1), (1, 0), (1, 1))
CELLS = [(1 + a, 1 + b) for a, b in OWN] + [(0, 0), (0, 1), (0, 2), (1, 0), (2, 0)]


def selection():
    result = np.zeros((3, 2, 2, 4, 16, 7, LANES), np.float32)
    for offset in range(3):
        for dx, (pair, odd) in enumerate(((1, 1), (0, 0), (0, 1))):
            for channel in range(4):
                for cell in range(7):
                    for dy in range(3):
                        lane = offset * SLOT + (dx * 3 + dy) * 4 + channel
                        result[offset, pair, odd, channel, 2 * cell + dy + 1, cell, lane] = 1
    return result.reshape(768, 7 * LANES)


def gelu_parts(v):
    square = v * v
    t = jnp.tanh(np.sqrt(2 / np.pi) * (v + 0.044715 * (v * square)))
    return t, square


def gelu(v):
    t, _ = gelu_parts(v)
    return 0.5 * v * (1 + t)


def gelu_slope(v):
    t, square = gelu_parts(v)
    return 0.5 * (1 + t) + 0.5 * v * (1 - t * t) * (np.sqrt(2 / np.pi) * (1 + 3 * 0.044715 * square))


def dot(a, b, transposed=False):
    return lax.dot_general(a, b, (((1,), (1 if transposed else 0,)), ((), ())), preferred_element_type=WIDE)


def down(v, period):
    row = lax.broadcasted_iota(jnp.int32, v.shape, 0)
    return jnp.where((row & (period - 1)) == 0, 0.0, pltpu.roll(v, 1, axis=0))


def up(v):
    row = lax.broadcasted_iota(jnp.int32, v.shape, 0)
    return jnp.where(row == v.shape[0] - 1, 0.0, pltpu.roll(v, v.shape[0] - 1, axis=0))


class Place:
    def __init__(self, dp, sx, sy):
        self.chips_x = min(4, sy // CORES)
        self.low_z, self.chips_y = sx, dp
        self.shift_y, self.shift_z = dp.bit_length() - 1, sx.bit_length() - 1
        self.plane = self.chips_x * dp
        self.depth = sx * (sy // (CORES * self.chips_x))
        self.y, self.sx, self.sy = (lax.axis_index(name) for name in ("dp", "sx", "sy"))
        self.core = lax.rem(self.sy, CORES)
        self.p = lax.rem(self.sy // CORES, self.chips_x) * dp + self.y
        self.mixed = CORES * self.chips_x
        self.t = lax.rem(self.sy, self.mixed)
        self.z = (self.sy // self.mixed) * sx + self.sx

    def device(self, core=None, p=None, z=None):
        core = self.core if core is None else core
        p = self.p if p is None else p
        z = self.z if z is None else z
        chip_x, y = p >> self.shift_y, p & (self.chips_y - 1)
        high, low = z >> self.shift_z, z & (self.low_z - 1)
        return (y, low, (high * self.chips_x + chip_x) * CORES + core)


def others(count, me, body):
    for distance in sorted(range(1, count), key=lambda step: -min(step, count - step)):
        body((me + distance) & (count - 1))


def copy(source, target, sems, at, there, device):
    return pltpu.make_async_remote_copy(
        src_ref=source, dst_ref=target, send_sem=sems.at[0, at], recv_sem=sems.at[1, there],
        device_id=device, device_id_type=MESH)


class Reduction:
    def __init__(self, here, grads, refs, direct):
        self.here, self.grads, self.direct = here, grads, direct
        (self.half_out, self.half_in, self.plane_out, self.plane_in, self.depth_out, self.depth_in,
         self.final, self.gathered, self.half_sems, self.plane_sems, self.depth_sems, self.final_sems,
         self.gather_sems, self.pair_sems) = refs
        self.share = self.plane_out.shape[1]
        self.half = here.plane * self.share
        self.partner = here.device(core=1 - here.core)
        owners = [unit * here.depth // self.share for unit in range(self.share)]
        self.owned = [] if direct else [(unit, owner, unit - owners.index(owner)) for unit, owner in enumerate(owners)]

    @staticmethod
    def scratch(units, plane, depth, direct):
        share = units // (CORES * plane)
        slots = share if direct else -(-share // depth)
        unit = (ROWS, LANES)
        return [
            pltpu.VMEM((plane * share, *unit), LOW),
            pltpu.VMEM((plane * share, *unit), LOW),
            pltpu.VMEM((plane, share, *unit), LOW),
            pltpu.VMEM((plane, share, *unit), LOW),
            pltpu.VMEM((share, *unit), LOW),
            pltpu.VMEM((depth, slots, *unit) if direct else (slots, depth, *unit), LOW),
            pltpu.VMEM((share, *unit), LOW),
            pltpu.VMEM((CORES, plane, share, *unit), LOW),
            pltpu.SemaphoreType.DMA((2, 1)),
            pltpu.SemaphoreType.DMA((2, plane)),
            pltpu.SemaphoreType.DMA((2, max(share, slots * depth))),
            pltpu.SemaphoreType.DMA((2, max(share, slots * depth))),
            pltpu.SemaphoreType.DMA((2, plane)),
            pltpu.SemaphoreType.DMA((2, plane)),
        ]

    def swap(self):
        return copy(self.half_out, self.half_in, self.half_sems, 0, 0, self.partner)

    def start_swap(self):
        self.half_out[...] = self.grads[pl.ds((1 - self.here.core) * self.half, self.half)].astype(LOW)
        self.swap().start()

    def to_plane(self, q, source_slot):
        here = self.here
        return copy(self.plane_out.at[q], self.plane_in.at[source_slot], self.plane_sems, q, source_slot, here.device(p=q))

    def start_plane(self):
        here = self.here
        self.swap().wait()
        if self.grads.shape[0] == self.half:
            mine = self.grads[...]
        else:
            mine = self.grads[pl.ds(here.core * self.half, self.half)]
        self.plane_out[...] = (mine + self.half_in[...].astype(WIDE)).astype(LOW).reshape(self.plane_out.shape)
        others(here.plane, here.p, lambda q: self.to_plane(q, here.p).start())

    def to_depth(self, unit, owner, slot, q):
        here = self.here
        return copy(self.depth_out.at[unit], self.depth_in.at[slot, q], self.depth_sems, unit,
                    slot * here.depth + q, here.device(z=owner))

    def start_depth(self):
        here = self.here
        self.plane_in[here.p] = self.plane_out[here.p]
        others(here.plane, here.p, lambda q: self.to_plane(q, q).wait())
        self.depth_out[...] = jnp.sum(self.plane_in[...].astype(WIDE), axis=0).astype(LOW)
        if self.direct:
            others(here.depth, here.z, lambda q: self.to_all(q, here.z).start())
            return
        for unit, owner, slot in self.owned:
            @pl.when(here.z != owner)
            def _():
                self.to_depth(unit, owner, slot, here.z).start()

    def to_all(self, q, source_slot):
        here = self.here
        return copy(self.depth_out, self.depth_in.at[source_slot], self.depth_sems, q, source_slot, here.device(z=q))

    def to_final(self, unit, slot, q):
        here = self.here
        return copy(self.final.at[unit], self.final.at[unit], self.final_sems, slot * here.depth + q, unit, here.device(z=q))

    def start_final(self):
        here = self.here
        for unit, owner, slot in self.owned:
            @pl.when(here.z == owner)
            def _():
                self.depth_in[slot, owner] = self.depth_out[unit]
                others(here.depth, here.z, lambda q: self.to_depth(unit, q, slot, q).wait_recv())
                self.final[unit] = jnp.sum(self.depth_in[slot].astype(WIDE), axis=0).astype(LOW)
                others(here.depth, here.z, lambda q: self.to_final(unit, slot, q).start())

    def to_gather(self, q, source_slot):
        here = self.here
        return copy(self.final, self.gathered.at[here.core, source_slot], self.gather_sems, q, source_slot, here.device(p=q))

    def to_pair(self, core, q):
        return copy(self.gathered.at[core, q], self.gathered.at[core, q], self.pair_sems, q, q, self.partner)

    def start_gather(self):
        here = self.here
        if self.direct:
            self.depth_in[here.z] = self.depth_out[...]
            others(here.depth, here.z, lambda q: self.to_all(q, q).wait())
            self.final[...] = jnp.sum(self.depth_in[...].astype(WIDE), axis=0).astype(LOW)
        for unit, owner, slot in self.owned:
            @pl.when(here.z != owner)
            def _():
                self.to_depth(unit, owner, slot, here.z).wait_send()
                self.to_final(unit, slot, owner).wait_recv()

        others(here.plane, here.p, lambda q: self.to_gather(q, here.p).start())
        self.gathered[here.core, here.p] = self.final[...]
        self.to_pair(here.core, here.p).start()

    def pass_on(self):
        here = self.here

        def step(q):
            self.to_gather(q, q).wait_recv()
            self.to_pair(here.core, q).start()

        others(here.plane, here.p, step)

    def finish(self):
        here = self.here
        for unit, owner, slot in self.owned:
            @pl.when(here.z == owner)
            def _():
                others(here.depth, here.z, lambda q: self.to_final(unit, slot, q).wait_send())

        others(here.plane, here.p, lambda q: self.to_gather(q, q).wait_send())

        for q in range(here.plane):
            self.to_pair(1 - here.core, q).wait()
        return self.gathered[...].reshape(-1, ROWS, LANES)


class Halo:
    def __init__(self, here, sizes, step, sems, first, triples, needs=None):
        self.items = []
        for index, (along_x, along_y, source, target) in enumerate(triples):
            sends = receives = needs
            for along, place, size in ((along_x, here.sx, sizes[1]), (along_y, here.sy, sizes[2])):
                if not along:
                    continue
                ahead, behind = place < size - 1, place > 0
                send, receive = (ahead, behind) if step > 0 else (behind, ahead)
                sends = send if sends is None else jnp.logical_and(sends, send)
                receives = receive if receives is None else jnp.logical_and(receives, receive)
            device = (here.y, here.sx + step * along_x, here.sy + step * along_y)
            move = copy(source, target, sems, first + index, first + index, device)
            self.items.append((sends, receives, move, target))

    def start(self, first=0, last=None):
        for sends, _, move, _ in self.items[first:last]:
            @pl.when(sends)
            def _():
                move.start()

    def wait(self, first=0, last=None):
        for _, receives, move, target in self.items[first:last]:
            @pl.when(receives)
            def _():
                move.wait_recv()

            @pl.when(jnp.logical_not(receives))
            def _():
                target[...] = jnp.zeros(target.shape, target.dtype)

    def sent(self):
        for sends, _, move, _ in self.items:
            @pl.when(sends)
            def _():
                move.wait_send()


def kernel(sizes, volume_hbm, cotangent_hbm, w1_hbm, w2, w3, select, sum_a, sum_b,
           volume, vx, vy, vc, cotangent, w1, w1c, w2s, w3s, sel, local_sems, halo_sems, s1, r1, r1_sems, s2, r2, r2_sems,
           dts, xoff, c1, g1, act1, act1s, lhs2, pre2, g2, g2x, g2y, g2x_in, g2y_in, g2c_in, lhs3, d3, d3x, d3y, d3c,
           lhs2t, c1t, d2s, d1, grads_a, grads_b, *reductions):
    here = Place(*sizes)
    _, size_x, size_y = sizes
    mixed, depth = here.mixed, here.depth
    kept, high = cotangent.shape[0], size_y // mixed

    barrier = pltpu.get_barrier_semaphore()

    def greet(device):
        pl.semaphore_signal(barrier, inc=1, device_id=device, device_id_type=MESH)

    def at_mixed(t):
        return (here.y, here.sx, here.sy - here.t + t)

    expected = depth + mixed + here.plane - 3
    for along_x in range(2):
        for step in (-1, 1):
            inside = here.sy > 0 if step < 0 else here.sy < size_y - 1
            if along_x:
                inside = jnp.logical_and(inside, here.sx > 0 if step < 0 else here.sx < size_x - 1)
            expected = expected + inside.astype(jnp.int32)

            @pl.when(inside)
            def _():
                greet((here.y, here.sx + step * along_x, here.sy + step))

    others(depth, here.z, lambda q: greet(here.device(z=q)))
    others(mixed, here.t, lambda q: greet(at_mixed(q)))
    others(here.plane, here.p, lambda q: greet(here.device(p=q)))
    loads = [
        pltpu.make_async_copy(w1_hbm, w1.at[pl.ds(0, 3)], local_sems.at[0]),
        pltpu.make_async_copy(cotangent_hbm, cotangent, local_sems.at[1]),
        pltpu.make_async_copy(volume_hbm, volume, local_sems.at[2]),
        pltpu.make_async_copy(select, sel, local_sems.at[3]),
        pltpu.make_async_copy(w2.at[:, :, pl.ds(1, 2)], w2s.at[:, :, pl.ds(0, 2)], local_sems.at[4]),
        pltpu.make_async_copy(w2.at[:, :, pl.ds(0, 1)], w2s.at[:, :, pl.ds(3, 1)], local_sems.at[5]),
        pltpu.make_async_copy(w3.at[:, :, pl.ds(1, 2)], w3s.at[:, :, pl.ds(0, 2)], local_sems.at[6]),
        pltpu.make_async_copy(w3.at[:, :, pl.ds(0, 1)], w3s.at[:, :, pl.ds(3, 1)], local_sems.at[7]),
    ]
    for load in loads:
        load.start()
    for ref in (w2s, w3s):
        ref[:, :, 2] = jnp.zeros((3, 3, *ref.shape[3:]), LOW)
    for index in range(8):
        dts[index, 0:8, :] = jnp.zeros((8, 128), WIDE)
    w1c[...] = jnp.zeros(w1c.shape, WIDE)
    blank = jnp.zeros((4, 64), WIDE)

    loads[0].wait()
    for offset in range(5):
        base = offset * SLOT if offset < 3 else 128 + (offset - 3) * SLOT
        for dx in range(3):
            for dy in range(3):
                left = w1[dx, dy, offset].astype(WIDE) if offset <= 2 else blank
                right = w1[dx, dy, offset - 2].astype(WIDE) if offset >= 2 else blank
                w1c[pl.ds(base + (dx * 3 + dy) * 4, 4), :] = jnp.concatenate([left, right], axis=1)

    loads[1].wait()
    spread = size_x * kept * ROWS
    lane = lax.broadcasted_iota(jnp.int32, (ROWS, spread), 1)
    row = lax.broadcasted_iota(jnp.int32, (ROWS, spread), 0)
    repeat = jnp.where((lane & (ROWS - 1)) == row, 1.0, 0.0).astype(LOW)
    wide = dot(cotangent[...].reshape(kept * size_x * size_y, ROWS), repeat).reshape(kept * size_x, size_y, spread)
    lane = lax.broadcasted_iota(jnp.int32, wide.shape, 2)
    group = lax.broadcasted_iota(jnp.int32, wide.shape, 0)
    strips = jnp.sum(jnp.where((lane >> 4) == lax.rem(group, size_x) * kept + group // size_x, wide, 0.0), axis=0)
    rows = 8 // high
    for t in range(mixed):
        for part in range(high):
            y = part * mixed + t
            s1[t, part * rows:(part + 1) * rows, :] = jnp.broadcast_to(strips[y:y + 1, :], (rows, spread))

    loads[2].wait()
    pl.semaphore_wait(barrier, expected)
    pieces = [pl.ds(64 * channel, 64) for channel in range(4)]
    volumes = Halo(here, sizes, 1, halo_sems, 0, (
        *((0, 1, volume.at[piece], vy.at[piece]) for piece in pieces), (1, 0, volume, vx)))
    corners = Halo(here, sizes, 1, halo_sems, 5, [(1, 0, vy.at[piece], vc.at[piece]) for piece in pieces], here.sy > 0)
    volumes.start()

    def to_mixed(q, source_slot):
        return copy(s1.at[q], r1.at[source_slot], r1_sems, q, source_slot, at_mixed(q))

    def to_cell(q, source_slot):
        return copy(s2.at[q], r2.at[source_slot], r2_sems, q, source_slot, here.device(z=q))

    others(mixed, here.t, lambda q: to_mixed(q, here.t).start())
    r1[here.t] = s1[here.t]
    others(mixed, here.t, lambda q: to_mixed(q, q).wait())
    for part in range(high):
        strips = jnp.max(r1[:, part * rows:(part + 1) * rows, :], axis=1)
        for x in range(size_x):
            s2[part * size_x + x] = strips[:, x * kept * ROWS:(x + 1) * kept * ROWS]
    others(depth, here.z, lambda q: to_cell(q, here.z).start())
    r2[here.z] = s2[here.z]

    for part in range(4):
        volumes.wait(part, part + 1)
        corners.start(part, part + 1)
    loads[3].wait()
    volumes.wait(4)
    corners.wait()

    for pair in range(8):
        before, inside = (vc, vx) if pair < 4 else (vy, volume)
        tiles = []
        for channel in range(4):
            at = channel * 64 + (pair % 4) * 16
            tiles.append([ref[at:at + 16, :].astype(WIDE) for ref in (before, inside)])
        ordered = [both[odd * 8:(odd + 1) * 8] for odd in range(2) for refs in tiles for both in refs]
        dts[pair, 8:136, :] = jnp.concatenate(ordered, axis=0).T
    for offset in range(5):
        for pair in range(8):
            xoff[offset, pair * 32:(pair + 1) * 32, :] = dts[pair, pl.ds(7 + offset, 32, stride=4), :].astype(LOW)
    for part, offsets in enumerate(((0, 1, 2), (3, 4))):
        blocks = []
        for offset in offsets:
            blocks += [xoff[offset, 32:256, :], xoff[offset, 0:224, :]]
        chosen = dot(jnp.concatenate(blocks, axis=1), sel[0:256 * len(offsets), :])
        for cell in range(7):
            c1[cell, :, part * 128:(part + 1) * 128] = chosen[:, cell * 128:(cell + 1) * 128].astype(LOW)
    first = w1c[...].astype(LOW)
    for cell in range(7):
        pre = dot(c1[cell], first)
        if cell >= 3:
            g1[cell - 3] = gelu_slope(pre[96:224])
        act = gelu(pre)
        act1[cell] = act.astype(LOW)
        act1s[cell] = down(act, 32).astype(LOW)

    for index, (x, y) in enumerate(CELLS):
        for dx in range(3):
            for dy in range(3):
                at = (dx * 3 + dy) * 256
                rows = slice((2 * x + dx) * 32, (2 * x + dx + 1) * 32)
                lhs2[index * 32:(index + 1) * 32, at:at + 128] = act1[2 * y + dy, rows, :]
                lhs2[index * 32:(index + 1) * 32, at + 128:at + 256] = act1s[2 * y + dy, rows, :]
    for load in loads[4:6]:
        load.wait()
    second = w2s[...].reshape(2304, 64)
    pre2[...] = dot(lhs2[...], second)
    for index, (x, y) in enumerate(CELLS):
        pre = jnp.concatenate(
            [pre2[pl.ds(index * 32 + parity, 16, stride=2), :] for parity in range(2)], axis=1)
        if index < 4:
            slope = gelu_slope(pre)
            g2[index] = slope
            if index < 2:
                g2x[index] = slope.astype(LOW)
            if index in (0, 2):
                g2y[index // 2] = slope.astype(LOW)
        act = gelu(pre)
        at = (x * 3 + y) * 256
        lhs3[:, at:at + 128] = act
        lhs3[:, at + 128:at + 256] = down(act, 16)
    slopes = Halo(here, sizes, -1, halo_sems, 9, (
        (0, 1, g2y, g2y_in), (1, 1, g2x.at[pl.ds(0, 1)], g2c_in), (1, 0, g2x, g2x_in)))
    slopes.start()

    others(depth, here.z, lambda q: to_cell(q, q).wait())
    strips = r2[...].reshape(depth * mixed, kept * ROWS).T.astype(LOW)
    sender = lax.broadcasted_iota(jnp.int32, (depth * mixed, 256), 0)
    channel = lax.broadcasted_iota(jnp.int32, (depth * mixed, 256), 1)
    z, t = sender // mixed, lax.rem(sender, mixed)
    channel = channel - ((lax.rem(z, size_x) * size_y + (z // size_x) * mixed + t) * kept)
    upstream = 0.0
    for k in range(kept):
        choose = jnp.where(channel == k, 1.0, 0.0).astype(LOW)
        upstream = upstream + dot(strips[k * ROWS:(k + 1) * ROWS], choose)
    for load in loads[6:8]:
        load.wait()
    third = w3s[...].reshape(2304, 256)
    pre = dot(lhs3[...].astype(LOW), third)
    delta = (gelu_slope(pre) * upstream).astype(LOW)
    d3[...] = delta
    deltas = Halo(here, sizes, -1, halo_sems, 12, ((0, 1, d3, d3y), (1, 1, d3, d3c), (1, 0, d3, d3x)))
    deltas.start()

    many = len(reductions) // 2
    large = Reduction(here, grads_a, reductions[:many], False)
    small = Reduction(here, grads_b, reductions[many:], True)
    turned = [lhs3[:, tap * 256:(tap + 1) * 256].T.astype(LOW) for tap in range(9)]
    halves = [delta[:, lanes * 128:(lanes + 1) * 128].astype(WIDE) for lanes in range(2)]
    even = here.core == 0

    def third_grad(right, target):
        for tap in range(9):
            grad = dot(turned[tap], right.astype(LOW))
            for dz, rows in enumerate((192, 0, 64)):
                at = (tap * 3 + dz) * 4
                target[at:at + 4] = grad[rows:rows + 64].astype(target.dtype).reshape(4, ROWS, LANES)
        spare = target.shape[0] - THIRD_UNITS // 2
        if spare:
            target[THIRD_UNITS // 2:] = jnp.zeros((spare, ROWS, LANES), target.dtype)

    third_grad(jnp.where(even, halves[1], halves[0]), large.half_out)
    large.swap().start()
    third_grad(jnp.where(even, halves[0], halves[1]), grads_a)

    for block in range(18):
        lhs2t[block * 128:(block + 1) * 128, :] = lhs2[0:128, block * 128:(block + 1) * 128].astype(WIDE).T.astype(LOW)
    for cell in range(4):
        for half in range(2):
            lanes = slice(half * 128, (half + 1) * 128)
            c1t[lanes, cell * 128:(cell + 1) * 128] = c1[3 + cell, 96:224, lanes].astype(WIDE).T.astype(LOW)

    large.start_plane()
    slopes.wait()
    deltas.wait()

    sources = {(0, 0): 0, (1, 0): 1, (0, 1): 2, (1, 1): 3}
    back = dot(jnp.concatenate([d3[...], d3x[...], d3y[...], d3c[...]], axis=0), third, transposed=True)
    reads = {0: ((0, 1),), 1: ((0, 2), (1, 0)), 2: ((1, 1),)}
    slope_at = {(0, 0): g2.at[0], (0, 1): g2.at[1], (1, 0): g2.at[2], (1, 1): g2.at[3],
                (2, 0): g2x_in.at[0], (2, 1): g2x_in.at[1], (0, 2): g2y_in.at[0], (1, 2): g2y_in.at[1],
                (2, 2): g2c_in.at[0]}
    for a in range(3):
        for b in range(3):
            total = 0.0
            for from_x, dx in reads[a]:
                for from_y, dy in reads[b]:
                    at, tap = sources[from_x, from_y] * 16, (dx * 3 + dy) * 256
                    total = total + back[at:at + 16, tap:tap + 256]
            value = slope_at[a, b][...].astype(WIDE) * (total[:, 0:128] + up(total[:, 128:256]))
            d2s[a * 3 + b, pl.ds(0, 16, stride=2), :] = value[:, 0:64]
            d2s[a * 3 + b, pl.ds(1, 16, stride=2), :] = value[:, 64:128]

    delta = jnp.concatenate([d2s[a * 3 + b].astype(LOW) for a, b in OWN], axis=0)
    grad = dot(lhs2t[...], delta)

    def second_block(block):
        if block > 26:
            return jnp.zeros((64, 64), WIDE)
        start = (block // 3) * 256 + (192, 0, 64)[block % 3]
        return grad[start:start + 64]

    for block in range(14):
        both = jnp.concatenate([second_block(block), second_block(block + 14)], axis=1)
        grads_b[block * 4:(block + 1) * 4] = both.reshape(4, ROWS, LANES)

    sums = {}
    for dx in range(3):
        for dy in range(3):
            cells = [((1 if dx == 0 else 0) + a, (1 if dy == 0 else 0) + b) for a, b in OWN]
            stacked = jnp.concatenate([d2s[a * 3 + b].astype(LOW) for a, b in cells], axis=0)
            tap = (dx * 3 + dy) * 256
            back = dot(stacked, second[tap:tap + 256], transposed=True)
            for index, (a, b) in enumerate(cells):
                place = (2 * a + dx - 1, 2 * b + dy - 1)
                part = back[index * 32:(index + 1) * 32]
                sums[place] = sums[place] + part if place in sums else part
    for a in range(4):
        for b in range(4):
            total = sums[a, b]
            value = g1[b, a * 32:(a + 1) * 32] * (total[:, 0:128] + up(total[:, 128:256]))
            d1[b * 128 + a * 32:b * 128 + (a + 1) * 32, :] = value.astype(LOW)
    grad = dot(c1t[...], d1[...])
    for dz in range(3):
        start = (0, SLOT, 2 * SLOT)[dz]
        other = (2 * SLOT, 128, 128 + SLOT)[dz]
        w1c[dz * SLOT:(dz + 1) * SLOT, :] = jnp.concatenate(
            [grad[start:start + SLOT, 0:64] + grad[other:other + SLOT, 64:128], jnp.zeros((SLOT, 64), WIDE)], axis=1)
    w1c[120:128, :] = jnp.zeros((8, 128), WIDE)
    grads_b[SECOND_UNITS:SECOND_UNITS + FIRST_UNITS] = w1c[0:128, :].reshape(FIRST_UNITS, ROWS, LANES)

    small.start_swap()
    large.start_depth()
    small.start_plane()
    large.start_final()
    small.start_depth()
    large.start_gather()
    small.start_gather()
    large.pass_on()
    small.pass_on()
    sum_a[...] = large.finish()
    sum_b[...] = small.finish()
    volumes.sent()
    corners.sent()
    slopes.sent()
    deltas.sent()


def unpack_kernel(sum_a, sum_b, out1, out2, out3, first, second, third, sems):
    half = sum_a.shape[0] // 2
    copies = []
    for part in range(3):
        for lanes in range(2):
            at = lanes * half + part * 36
            block = sum_a[at:at + 36].reshape(576, LANES)
            third[part * 576:(part + 1) * 576, lanes * 128:(lanes + 1) * 128] = block.astype(WIDE)
        rows = pl.ds(part * 576, 576)
        copies.append(pltpu.make_async_copy(third.at[rows], out3.at[rows], sems.at[part]))
        copies[part].start()
    both = sum_b[0:SECOND_UNITS].reshape(896, LANES).astype(WIDE)
    second[0:896, :] = both[:, 0:64]
    second[896:1728, :] = both[0:832, 64:128]
    copies.append(pltpu.make_async_copy(second, out2, sems.at[3]))
    copies[3].start()
    rows = sum_b[SECOND_UNITS:SECOND_UNITS + FIRST_UNITS].reshape(128, LANES).astype(WIDE)
    for dx in range(3):
        for dy in range(3):
            for dz in range(3):
                at = dz * SLOT + (dx * 3 + dy) * 4
                first[dx, dy, dz] = rows[at:at + 4, 0:64]
    copies.append(pltpu.make_async_copy(first.at[pl.ds(0, 3)], out1, sems.at[4]))
    copies[4].start()
    for move in copies:
        move.wait()


def unpacked(sums):
    whole, far = pl.BlockSpec(memory_space=pltpu.VMEM), pl.BlockSpec(memory_space=pltpu.HBM)
    shapes = ((3, 3, 3, 4, 64), (1728, 64), (1728, 256))
    return pl.pallas_call(
        unpack_kernel,
        out_shape=tuple(jax.ShapeDtypeStruct(shape, WIDE) for shape in shapes),
        in_specs=[whole] * 2,
        out_specs=(far,) * 3,
        scratch_shapes=[*(pltpu.VMEM(shape, WIDE) for shape in ((4, *shapes[0][1:]), *shapes[1:])), pltpu.SemaphoreType.DMA((5,))],
        compiler_params=pltpu.CompilerParams(vmem_limit_bytes=16 * 2**20),
    )(*sums)


def local(sizes, volume, cotangent, first_weight, second_weight, third_weight):
    dp, size_x, size_y = sizes
    plane = min(4, size_y // CORES) * dp
    depth = size_x * (size_y // (CORES * min(4, size_y // CORES)))
    grain = CORES * plane
    units_a = -(-THIRD_UNITS // grain) * grain
    units_b = -(-(FIRST_UNITS + SECOND_UNITS) // grain) * grain
    kept = cotangent.shape[1]
    spread = size_x * kept * ROWS
    vmem, sems = pltpu.VMEM, pltpu.SemaphoreType.DMA
    mixed = CORES * min(4, size_y // CORES)
    whole, far = pl.BlockSpec(memory_space=pltpu.VMEM), pl.BlockSpec(memory_space=pltpu.HBM)
    sums = pl.pallas_call(
        functools.partial(kernel, sizes),
        out_shape=(pltpu.VMEM((units_a, ROWS, LANES), LOW), pltpu.VMEM((units_b, ROWS, LANES), LOW)),
        in_specs=[far] * 6,
        out_specs=(whole, whole),
        scratch_shapes=[
            vmem((256, 128), LOW), vmem((256, 128), LOW), vmem((256, 128), LOW), vmem((256, 128), LOW),
            vmem(cotangent.shape[1:], LOW), vmem((4, *first_weight.shape[1:]), LOW), vmem((256, 128), WIDE), vmem((3, 3, 4, 64, 64), LOW), vmem((3, 3, 4, 64, 256), LOW), vmem((768, 896), LOW),
            sems((8,)), sems((2, 15)),
            vmem((mixed, 8, spread), WIDE), vmem((mixed, 8, spread), WIDE), sems((2, mixed)),
            vmem((depth, mixed, kept * ROWS), WIDE), vmem((depth, mixed, kept * ROWS), WIDE), sems((2, depth)),
            vmem((8, 136, 128), WIDE), vmem((5, 256, 128), LOW), vmem((7, 224, 256), LOW), vmem((4, 128, 128), WIDE),
            vmem((7, 224, 128), LOW), vmem((7, 224, 128), LOW), vmem((288, 2304), LOW), vmem((288, 64), WIDE),
            vmem((4, 16, 128), WIDE), vmem((2, 16, 128), LOW), vmem((2, 16, 128), LOW),
            vmem((2, 16, 128), LOW), vmem((2, 16, 128), LOW), vmem((1, 16, 128), LOW),
            vmem((16, 2304), WIDE), vmem((16, 256), LOW), vmem((16, 256), LOW), vmem((16, 256), LOW), vmem((16, 256), LOW),
            vmem((2304, 128), LOW), vmem((256, 512), LOW), vmem((9, 32, 64), WIDE), vmem((512, 128), LOW),
            vmem((units_a // 2, ROWS, LANES), WIDE), vmem((units_b, ROWS, LANES), WIDE),
            *Reduction.scratch(units_a, plane, depth, False), *Reduction.scratch(units_b, plane, depth, True),
        ],
        compiler_params=pltpu.CompilerParams(collective_id=1, has_side_effects=True, vmem_limit_bytes=60 * 2**20),
        cost_estimate=pl.CostEstimate(flops=1_000_000_000, bytes_accessed=8_000_000, transcendentals=1_000_000),
    )(volume.reshape(256, 128), cotangent[0], first_weight, second_weight, third_weight, jnp.asarray(selection(), LOW))
    first, second, third = unpacked(sums)
    return first, second.reshape(3, 3, 3, 64, 64), third.reshape(3, 3, 3, 64, 256)


def solution(mesh):
    sizes = tuple(mesh.shape[name] for name in ("dp", "sx", "sy"))
    placed = (P("dp", None, "sx", "sy", None), P("dp", ("sx", "sy"), None, None, None), P(), P(), P())
    return jax.shard_map(
        functools.partial(local, sizes), mesh=mesh, in_specs=placed, out_specs=(P(), P(), P()), check_vma=False)
```
